1024 devices in a mesh: dp: 16 (over z, core), expert: 64 (over x, y).
Axes of the slice: x: 8, y: 8, z: 8, core: 2. Of those that a mesh axis runs over, the one named last changes fastest.
Arguments:
- tokens: bfloat16 [8192, 4096], P('expert', 'dp'), may hold values from -6 to 6
- routes: int32 [8192, 8], P('expert'), may hold values from 0 to 63, all different within a row; in each aligned block of 128 rows (0 to 127, 128 to 255, ...) at most 18 rows name the same one
- combine: float32 [8192, 8], P('expert'), may hold values from 0.05 to 0.5
- clip_mask: int32 [8192], P('expert'), may hold values 0 or 1
- limits: int32 [64], replicated, may hold values from 1 to 18, as said below
- cotangent: bfloat16 [8192, 4096], P('expert', 'dp'), may hold values from -6 to 6
- gate_weight: bfloat16 [64, 4096, 768], P('expert', 'dp'), may hold values from -0.09375 to 0.09375
- up_weight: bfloat16 [64, 4096, 768], P('expert', 'dp'), may hold values from -0.09375 to 0.09375
- down_weight: bfloat16 [64, 768, 4096], P('expert', None, 'dp'), may hold values from -0.21875 to 0.21875
Outputs:
- layer_out: bfloat16 [8192, 4096], P('expert', 'dp')
- token_grads: bfloat16 [8192, 4096], P('expert', 'dp')
- gate_grads: bfloat16 [64, 4096, 768], P('expert', 'dp')
- up_grads: bfloat16 [64, 4096, 768], P('expert', 'dp')
- down_grads: bfloat16 [64, 768, 4096], P('expert', None, 'dp')
The draws below stay inside these ranges and needn't reach their ends.
Inputs may be any that keep to these rules, and one draw needn't show every extreme that they name: `routes`: each token lists 8 different experts. Among the 128 tokens of one index of expert (an aligned block), no expert is listed more than 18 times, a bound that some block reaches. `limits`: some expert's limit is exactly 18.
All inputs are finite; a program needn't handle non-finite values. No bound on the sum of `clip_mask` on one device may be relied on, other than what follows from the above.
Results may differ from the reference program's by a relative error of at most 0.035.
Values may be sent and summed in bfloat16 or wider, within the bound.
No kernel may reach another device: no remote copies, remote signals or barrier semaphores. Data moves between devices by JAX's collectives and lax.ppermute only.
A program may use at most 64 MiB of HBM per device.

```python
import math
import jax
import jax.numpy as jnp
import numpy as np
from jax import lax

D = 4096
TOP = 8
FF = 768
EXPERTS = 64
TOK_DEV = 128
TOKENS = 8192
CAP = 18
N_DP = 16
N_EXPERT = 64


def draw_limits(key, part):
    key = jax.random.fold_in(key, 11)
    key_values, key_pick = jax.random.split(key)
    values = jax.random.randint(key_values, (EXPERTS,), 1, CAP + 1, dtype=jnp.int32)
    chosen = jax.random.randint(key_pick, (), 0, EXPERTS, dtype=jnp.int32)
    return jnp.where(jnp.arange(EXPERTS, dtype=jnp.int32) == chosen, CAP, values).astype(jnp.int32)


def place_ends(result, key, least, high):
    longest = result.shape.index(max(result.shape))
    spots = []
    for shift in (0, 1):
        where = [jax.random.randint(jax.random.fold_in(key, axis), (), 0, length) for axis, length in enumerate(result.shape)]
        where[longest] = (where[longest] + shift) % result.shape[longest]
        spots.append(tuple(where))
    return result.at[spots[0]].set(least).at[spots[1]].set(high)


def levels(own_key, dims, cuts, least, top_value):
    factor_of = 1.0
    for axis_at, parts in cuts:
        heights = jax.random.uniform(jax.random.fold_in(jax.random.fold_in(own_key, 6), axis_at), (parts,), jnp.float32, least / len(cuts), top_value / len(cuts))
        factor_of = factor_of * jnp.repeat(jnp.exp(heights), dims[axis_at] // parts).reshape((-1,) + (1,) * (len(dims) - 1 - axis_at))
    return factor_of


def routed_block(rng, own, number, rows, number_of, top, bound, lean):
    sequence = jax.random.permutation(rng, number_of)
    crowded, usual = portions_of(number_of, rows * top, bound, lean, True), portions_of(number_of, rows * top, bound, lean, False)
    places = jnp.arange(number_of)

    def named(tallies, turn):
        used = int((tallies > 0).sum())
        fixed = max(1, used // 4)
        shifted = fixed + (places - fixed + turn * (used - fixed)) % max(1, number_of - fixed)
        return jnp.zeros((number_of,), jnp.int32).at[sequence[jnp.where(places < fixed, places, shifted)]].set(jnp.asarray(tallies, jnp.int32))

    tallies = jnp.where(number % 4 == 0, named(crowded, number // 4), named(usual, number - number // 4 - 1))
    mixed = jax.random.permutation(jax.random.fold_in(own, 3), number_of)
    source_of, taker = mixed[0:number_of // 2 * 2:2], mixed[1:number_of // 2 * 2:2]
    room = jnp.minimum(tallies[source_of] - 1, bound - tallies[taker]) // 2
    room = jnp.where((source_of == sequence[0]) | (taker == sequence[0]) | (tallies[taker] == 0), 0, jnp.maximum(room, 0))
    shifted = jax.random.randint(jax.random.fold_in(own, 4), (number_of // 2,), 0, 1 << 20) % (room + 1)
    tallies = tallies.at[source_of].add(-shifted).at[taker].add(shifted)
    items = jnp.searchsorted(jnp.cumsum(tallies), jnp.arange(rows * top), side="right").astype(jnp.int32)
    listing = items.reshape(top, rows).T
    listing = listing[jax.random.permutation(jax.random.fold_in(own, 1), rows)]
    turn = jax.random.randint(jax.random.fold_in(own, 2), (rows, 1), 0, top)
    return jnp.take_along_axis(listing, (jnp.arange(top)[None, :] + turn) % top, axis=1)


def portions_of(count, total, bound, lean, full):
    loads = [(1 << 20) // math.isqrt(grade ** lean) + 1 for grade in range(1, count + 1)]
    largest = bound if full else min(bound, max(-(-total // count), total * loads[0] // sum(loads)))
    least = 1 if total - largest >= count - 1 else 0
    given, spare = [largest] + [least] * (count - 1), total - largest - least * (count - 1)
    while spare > 0:
        movable = [i for i in range(1, count) if given[i] < largest] or [i for i in range(1, count) if given[i] < bound]
        mass, budget = sum([loads[i] for i in movable]), spare
        for i in movable:
            extra = min(bound - given[i], max(1, budget * loads[i] // mass), spare)
            given[i] = given[i] + extra
            spare = spare - extra
    return np.array(given)


def bell_draw(own_key, dims, scale, limit, cuts=(), kind=jnp.bfloat16):
    loudness = levels(own_key, dims, cuts, -0.22, 0.18) if cuts else 1.0
    entries = jax.random.normal(own_key, dims, jnp.float32) * scale * loudness
    return jnp.minimum(jnp.maximum(entries, -limit), limit).astype(kind)


def setup_inputs(seed: int = 0) -> dict:
    arg_keys = jax.random.split(jax.random.key(seed), 10)
    tokens = bell_draw(arg_keys[0], (TOKENS, D), 1.0, 6.0, ((0, 64), (1, 16)))
    routes_keys = jax.random.split(jax.random.fold_in(arg_keys[1], 1), TOKENS // TOK_DEV)
    routes_turns = jax.random.permutation(jax.random.fold_in(arg_keys[1], 3), TOKENS // TOK_DEV)
    routes = jax.vmap(lambda own, number: routed_block(jax.random.fold_in(arg_keys[1], 2), own, number, TOK_DEV, EXPERTS, TOP, CAP, 2))(routes_keys, routes_turns).reshape((TOKENS, TOP))
    combine = jnp.clip(jnp.exp(math.log(0.5) - 2.3025851 * jax.random.uniform(arg_keys[2], (TOKENS, TOP), jnp.float32) ** levels(arg_keys[2], (TOKENS, TOP), ((0, 64),), -0.2, 0.2)), 0.05, 0.5)
    clip_mask = place_ends((jax.random.randint(arg_keys[3], (TOKENS,), 0, 4) < 3).astype(jnp.int32), jax.random.fold_in(arg_keys[3], 1), 0, 1)
    limits = draw_limits(jax.random.fold_in(arg_keys[9], 71), 0)
    cotangent = bell_draw(arg_keys[5], (TOKENS, D), 1.0, 6.0, ((0, 64), (1, 16)))
    gate_weight = bell_draw(arg_keys[6], (EXPERTS, D, FF), D ** -0.5, 0.09375, ((0, 64), (1, 16)))
    up_weight = bell_draw(arg_keys[7], (EXPERTS, D, FF), D ** -0.5, 0.09375, ((0, 64), (1, 16)))
    down_weight = bell_draw(arg_keys[8], (EXPERTS, FF, D), FF ** -0.5, 0.21875, ((0, 64), (2, 16)))
    return {"tokens": tokens, "routes": routes, "combine": combine, "clip_mask": clip_mask, "limits": limits, "cotangent": cotangent, "gate_weight": gate_weight, "up_weight": up_weight, "down_weight": down_weight}


def swish_parts(gate_val):
    sigma = jax.nn.sigmoid(gate_val)
    return gate_val * sigma, sigma * (1.0 + gate_val * (1.0 - sigma))


def block_sum(rows, weight):
    piece_width = rows.shape[1] // N_DP
    pieces = rows.astype(jnp.float32).reshape(rows.shape[0], N_DP, piece_width)
    blocks = weight.astype(jnp.float32).reshape(N_DP, piece_width, weight.shape[1])
    block_terms = jnp.einsum("rbd,bdf->brf", pieces, blocks, precision=lax.Precision.HIGHEST)
    rounded = lax.optimization_barrier(block_terms.astype(jnp.bfloat16))
    return jnp.sum(rounded.astype(jnp.float32), axis=0)


def slot_places(routes, limits):
    flat_ids = routes.reshape(N_EXPERT, TOK_DEV * TOP)
    labels = jnp.arange(EXPERTS, dtype=jnp.int32)
    onehot = (flat_ids[:, :, None] == labels[None, None, :]).astype(jnp.int32)
    rank_ids = jnp.sum((jnp.cumsum(onehot, axis=1) - onehot) * onehot, axis=2).astype(jnp.int32)
    sources = jnp.arange(N_EXPERT, dtype=jnp.int32)[:, None]
    places = (flat_ids * (N_EXPERT * CAP) + sources * CAP + rank_ids).astype(jnp.int32)
    dropped = jnp.int32(EXPERTS * N_EXPERT * CAP)
    return jnp.where(rank_ids < limits[flat_ids], places, dropped).reshape(TOKENS, TOP)


def reference(tokens, routes, combine, clip_mask, limits, cotangent, gate_weight, up_weight, down_weight):
    places = slot_places(routes, limits)
    total_slots = EXPERTS * N_EXPERT * CAP
    token_ids = jnp.broadcast_to(jnp.arange(TOKENS, dtype=jnp.int32)[:, None], (TOKENS, TOP))
    table = jnp.full((total_slots,), TOKENS, jnp.int32).at[places.reshape(-1)].set(token_ids.reshape(-1), mode="drop")
    scaled = combine * clip_mask.astype(jnp.float32)[:, None]
    coef_table = jnp.zeros((total_slots,), jnp.float32).at[places.reshape(-1)].set(scaled.reshape(-1), mode="drop")
    padded_x = jnp.concatenate([tokens, jnp.zeros((1, D), jnp.bfloat16)], axis=0)
    padded_g = jnp.concatenate([cotangent, jnp.zeros((1, D), jnp.bfloat16)], axis=0)

    def expert_pass(inputs):
        index_rows, coef_rows, gate_mat, up_mat, down_mat = inputs
        token_rows = padded_x[index_rows]
        grad_rows = (coef_rows[:, None] * padded_g[index_rows].astype(jnp.float32)).astype(jnp.bfloat16)
        gate_val = block_sum(token_rows, gate_mat)
        up_val = block_sum(token_rows, up_mat)
        active, slope = swish_parts(gate_val)
        hidden = (active * up_val).astype(jnp.bfloat16)
        out_rows = jnp.dot(hidden, down_mat, preferred_element_type=jnp.float32).astype(jnp.bfloat16)
        grad_hidden = block_sum(grad_rows, down_mat.T)
        grad_up = (grad_hidden * active).astype(jnp.bfloat16)
        grad_gate = (grad_hidden * up_val * slope).astype(jnp.bfloat16)
        input_rows = (jnp.dot(grad_gate, gate_mat.T, preferred_element_type=jnp.float32)
                      + jnp.dot(grad_up, up_mat.T, preferred_element_type=jnp.float32)).astype(jnp.bfloat16)
        gate_grad = jnp.dot(token_rows.T, grad_gate, preferred_element_type=jnp.float32).astype(jnp.bfloat16)
        upper_grad = jnp.dot(token_rows.T, grad_up, preferred_element_type=jnp.float32).astype(jnp.bfloat16)
        lower_grad = jnp.dot(hidden.T, grad_rows, preferred_element_type=jnp.float32).astype(jnp.bfloat16)
        return out_rows, input_rows, gate_grad, upper_grad, lower_grad

    row_count = N_EXPERT * CAP
    out_all, input_all, gate_grads, up_grads, down_grads = lax.map(
        expert_pass,
        (table.reshape(EXPERTS, row_count), coef_table.reshape(EXPERTS, row_count), gate_weight, up_weight, down_weight))
    zero_row = jnp.zeros((1, D), jnp.bfloat16)
    out_pad = jnp.concatenate([out_all.reshape(total_slots, D), zero_row], axis=0)
    input_pad = jnp.concatenate([input_all.reshape(total_slots, D), zero_row], axis=0)
    layer_out = jnp.sum(combine[:, :, None] * out_pad[places].astype(jnp.float32), axis=1).astype(jnp.bfloat16)
    token_grads = jnp.sum(input_pad[places].astype(jnp.float32), axis=1).astype(jnp.bfloat16)
    return layer_out, token_grads, gate_grads, up_grads, down_grads
```

```python
import functools

import jax
import jax.numpy as jnp
from jax import lax
from jax.experimental import pallas as pl
from jax.experimental.pallas import tpu as pltpu
from jax.sharding import PartitionSpec as P

LOW = jnp.bfloat16
WIDE = jnp.float32


def swish_parts(gate_val):
    sigma = jax.nn.sigmoid(gate_val)
    return (gate_val * sigma, sigma * (1.0 + gate_val * (1.0 - sigma)))


def mul(left, right):
    return jnp.dot(left, right, preferred_element_type=WIDE)


def split_low(values):
    high = values.astype(LOW)
    return high, (values - high.astype(WIDE)).astype(LOW)


def dispatch_kernel(
    capacity,
    routes_ref,
    combine_ref,
    clip_ref,
    limits_ref,
    tokens_ref,
    cot_ref,
    tok_out,
    cot_out,
    rank_out,
    weight_out,
):
    top_count, tok_rows = routes_ref.shape
    experts = limits_ref.shape[0]
    labels = lax.broadcasted_iota(jnp.int32, (experts, tok_rows), 0)
    listed = jnp.zeros((experts, tok_rows), WIDE)
    weight = jnp.zeros((experts, tok_rows), WIDE)
    for entry in range(top_count):
        match = routes_ref[entry : entry + 1, :] == labels
        listed = jnp.where(match, 1.0, listed)
        weight = jnp.where(match, combine_ref[entry : entry + 1, :], weight)
    before = lax.broadcasted_iota(jnp.int32, (tok_rows, tok_rows), 0) < lax.broadcasted_iota(
        jnp.int32, (tok_rows, tok_rows), 1
    )
    rank = mul(listed.astype(LOW), jnp.where(before, 1.0, 0.0).astype(LOW))
    kept = (listed > 0.0) & (rank < limits_ref[...].astype(WIDE))
    rank = jnp.where(kept, rank, -1.0)
    rank_out[...] = rank
    weight_out[...] = weight
    slots = experts * capacity
    first = lax.broadcasted_iota(jnp.int32, (slots, experts), 1) * capacity
    offset = lax.broadcasted_iota(jnp.int32, (slots, experts), 0) - first
    owner = jnp.where((offset >= 0) & (offset < capacity), 1.0, 0.0).astype(LOW)
    place = lax.broadcasted_iota(jnp.int32, (slots, tok_rows), 0).astype(WIDE)
    place = place - capacity * jnp.floor((place + 0.5) * (1.0 / capacity))
    picked = mul(owner, rank.astype(LOW)) == place
    tok_out[...] = mul(jnp.where(picked, 1.0, 0.0).astype(LOW), tokens_ref[...]).astype(LOW)
    high, rest = split_low(weight * clip_ref[...].astype(WIDE))
    coef_high = jnp.where(picked, mul(owner, high), 0.0).astype(LOW)
    coef_rest = jnp.where(picked, mul(owner, rest), 0.0).astype(LOW)
    cot = cot_ref[...]
    cot_out[...] = (mul(coef_high, cot) + mul(coef_rest, cot)).astype(LOW)


def gather_kernel(capacity, rank_ref, weight_ref, pick_out, weight_out):
    experts, tok_rows = rank_ref.shape
    slots = experts * capacity
    first = lax.broadcasted_iota(jnp.int32, (experts, slots), 0) * capacity
    offset = lax.broadcasted_iota(jnp.int32, (experts, slots), 1) - first
    owner = jnp.where((offset >= 0) & (offset < capacity), 1.0, 0.0).astype(LOW)
    place = lax.broadcasted_iota(jnp.int32, (tok_rows, slots), 1).astype(WIDE)
    place = place - capacity * jnp.floor((place + 0.5) * (1.0 / capacity))
    picked = mul(rank_ref[...].T.astype(LOW), owner) == place
    pick_out[...] = jnp.where(picked, 1.0, 0.0).astype(LOW)
    high, rest = split_low(weight_ref[...].T)
    weight_out[0:tok_rows, :] = jnp.where(picked, mul(high, owner), 0.0).astype(LOW)
    weight_out[tok_rows:, :] = jnp.where(picked, mul(rest, owner), 0.0).astype(LOW)


def body(
    tokens, routes, combine, clip_mask, limits, cotangent, gate_weight, up_weight, down_weight
):
    tok_rows, top_count = routes.shape
    experts = limits.shape[0]
    capacity = 9 * tok_rows * top_count // (8 * experts)
    slots = experts * capacity
    half = slots // 2
    width = tokens.shape[1]
    ff = gate_weight.shape[2]
    devices = lax.axis_size("dp")
    chips = devices // 2
    core = lax.axis_index("dp") % 2
    column = [[2 * chip + which for chip in range(chips)] for which in range(2)]
    swap_pairs = [(device, device ^ 1) for device in range(devices)]

    def swap(values):
        return lax.ppermute(values, "dp", swap_pairs)

    def exchange(rows):
        return lax.all_to_all(
            rows.reshape(experts, capacity, width), "expert", split_axis=0, concat_axis=0, tiled=True
        ).reshape(slots, width)

    def halves(rows):
        keep = lax.dynamic_slice_in_dim(rows, core * half, half, axis=0)
        give = lax.dynamic_slice_in_dim(rows, (1 - core) * half, half, axis=0)
        return keep, swap(give)

    def whole(rows):
        mine, got = rows[:, :width], swap(rows[:, width:])
        return jnp.where(
            core == 0, jnp.concatenate([mine, got], axis=0), jnp.concatenate([got, mine], axis=0)
        )

    gu_own = jnp.concatenate([gate_weight[0], up_weight[0]], axis=1)
    down_own = down_weight[0]
    gu_pair = jnp.concatenate([gu_own, swap(gu_own)], axis=0)
    down_pair = jnp.concatenate([down_own, swap(down_own)], axis=1)

    token_send, grad_send, rank, weight = pl.pallas_call(
        functools.partial(dispatch_kernel, capacity),
        out_shape=(
            jax.ShapeDtypeStruct((slots, width), LOW),
            jax.ShapeDtypeStruct((slots, width), LOW),
            jax.ShapeDtypeStruct((experts, tok_rows), WIDE),
            jax.ShapeDtypeStruct((experts, tok_rows), WIDE),
        ),
        compiler_params=pltpu.CompilerParams(vmem_limit_bytes=32 * 1024 * 1024),
        name="dispatch",
    )(
        routes.T,
        combine.T,
        clip_mask.reshape(1, tok_rows),
        limits.reshape(experts, 1),
        tokens,
        cotangent,
    )
    token_keep, token_got = halves(exchange(token_send))
    token_rows = jnp.concatenate([token_keep, token_got], axis=1)
    gate_up = mul(token_rows, gu_pair).astype(LOW)
    shares = lax.psum_scatter(
        gate_up, "dp", scatter_dimension=0, tiled=True, axis_index_groups=column
    ).astype(WIDE)
    grad_keep, grad_got = halves(exchange(grad_send))
    grad_rows = jnp.concatenate([grad_keep, grad_got], axis=1)
    grad_part = (
        lax.dot_general(
            grad_rows, down_pair, (((1,), (1,)), ((), ())), preferred_element_type=WIDE
        )
        .astype(LOW)
        .reshape(chips, half // chips, ff)
    )
    grad_hidden = jnp.sum(
        lax.all_to_all(
            grad_part, "dp", split_axis=0, concat_axis=0, tiled=True, axis_index_groups=column
        ).astype(WIDE),
        axis=0,
    )
    gate_val, up_val = shares[:, :ff], shares[:, ff:]
    active, slope = swish_parts(gate_val)
    hidden = (active * up_val).astype(LOW)
    derived = jnp.concatenate(
        [(grad_hidden * up_val * slope).astype(LOW), (grad_hidden * active).astype(LOW)], axis=1
    )
    derived_full = lax.all_gather(derived, "dp", axis=0, tiled=True, axis_index_groups=column)
    hidden_full = lax.all_gather(hidden, "dp", axis=0, tiled=True, axis_index_groups=column)
    back_rows = exchange(whole(mul(hidden_full, down_pair).astype(LOW)))
    input_rows = lax.dot_general(
        derived_full, gu_pair, (((1,), (1,)), ((), ())), preferred_element_type=WIDE
    ).astype(LOW)
    grads_back = exchange(whole(input_rows))

    def outer(left, right):
        return lax.dot_general(
            left, right, (((0,), (0,)), ((), ())), preferred_element_type=WIDE
        )

    lower_got = swap(outer(hidden_full, grad_got).astype(LOW))
    down_grads = (outer(hidden_full, grad_keep) + lower_got.astype(WIDE)).astype(LOW)
    upper_got = swap(outer(token_got, derived_full).astype(LOW)).astype(WIDE)
    gate_grads = (outer(token_keep, derived_full[:, :ff]) + upper_got[:, :ff]).astype(LOW)
    up_grads = (outer(token_keep, derived_full[:, ff:]) + upper_got[:, ff:]).astype(LOW)

    picked, weights = pl.pallas_call(
        functools.partial(gather_kernel, capacity),
        out_shape=(
            jax.ShapeDtypeStruct((tok_rows, slots), LOW),
            jax.ShapeDtypeStruct((2 * tok_rows, slots), LOW),
        ),
        compiler_params=pltpu.CompilerParams(vmem_limit_bytes=32 * 1024 * 1024),
        name="gather",
    )(rank, weight)
    sums = mul(weights, back_rows)
    layer_out = (sums[:tok_rows] + sums[tok_rows:]).astype(LOW)
    token_grads = mul(picked, grads_back).astype(LOW)
    return (layer_out, token_grads, gate_grads[None], up_grads[None], down_grads[None])


def solution(mesh):
    in_specs = (
        P("expert", "dp"),
        P("expert", None),
        P("expert", None),
        P("expert"),
        P(),
        P("expert", "dp"),
        P("expert", "dp", None),
        P("expert", "dp", None),
        P("expert", None, "dp"),
    )
    out_specs = (
        P("expert", "dp"),
        P("expert", "dp"),
        P("expert", "dp", None),
        P("expert", "dp", None),
        P("expert", None, "dp"),
    )
    return jax.shard_map(body, mesh=mesh, in_specs=in_specs, out_specs=out_specs, check_vma=False)
```

```python
import functools

import jax
import jax.numpy as jnp
from jax import lax
from jax.experimental import pallas as pl
from jax.experimental.pallas import tpu as pltpu
from jax.sharding import PartitionSpec as P

LOW = jnp.bfloat16
WIDE = jnp.float32


def swish_parts(gate_val):
    sigma = jax.nn.sigmoid(gate_val)
    return (gate_val * sigma, sigma * (1.0 + gate_val * (1.0 - sigma)))


def mul(left, right):
    return jnp.dot(left, right, preferred_element_type=WIDE)


def split_low(values):
    high = values.astype(LOW)
    return high, (values - high.astype(WIDE)).astype(LOW)


def outer(left, right):
    return lax.dot_general(left, right, (((0,), (0,)), ((), ())), preferred_element_type=WIDE)


def against(left, right):
    return lax.dot_general(left, right, (((1,), (1,)), ((), ())), preferred_element_type=WIDE)


def number(shape, axis):
    return lax.broadcasted_iota(jnp.int32, shape, axis).astype(WIDE)


def low_if(condition):
    return jnp.where(condition, 1.0, 0.0).astype(LOW)


def remainder(values, step):
    return values - step * jnp.floor((values + 0.5) * (1.0 / step))


def owners(shape, slot_axis, chunk):
    offset = number(shape, slot_axis) - chunk * number(shape, 1 - slot_axis)
    return low_if((offset >= 0.0) & (offset < chunk))


def wanted(shape, slot_axis, pad):
    within = remainder(number(shape, slot_axis), 2 * pad)
    left = jnp.where(within < pad, within, -5.0)
    right = jnp.where(within >= pad, within - pad, -5.0)
    return left, right


def token_kernel(
    pad,
    routes_hbm,
    combine_hbm,
    limits_hbm,
    tokens_hbm,
    tok_out,
    rank_out,
    weight_out,
    routes_ref,
    combine_ref,
    limits_ref,
    tokens_ref,
    sems,
):
    copies = [
        pltpu.make_async_copy(source, target, sems.at[at])
        for at, (source, target) in enumerate(
            (
                (routes_hbm, routes_ref),
                (combine_hbm, combine_ref),
                (limits_hbm, limits_ref),
                (tokens_hbm, tokens_ref),
            )
        )
    ]
    for copy in copies:
        copy.start()
    top_count, tok_rows = routes_ref.shape
    experts = limits_ref.shape[1]
    chunk = 2 * pad
    slots = experts * chunk
    owner = owners((slots, experts), 0, chunk)
    left, right = wanted((slots, tok_rows), 0, pad)
    before = number((tok_rows, tok_rows), 0) < number((tok_rows, tok_rows), 1)
    square = (experts, experts)
    for copy in copies:
        copy.wait()
    labels = lax.broadcasted_iota(jnp.int32, (experts, tok_rows), 0)
    listed = jnp.zeros((experts, tok_rows), WIDE)
    weight = jnp.zeros((experts, tok_rows), WIDE)
    for entry in range(top_count):
        match = routes_ref[entry : entry + 1, :] == labels
        listed = jnp.where(match, 1.0, listed)
        weight = jnp.where(match, combine_ref[entry : entry + 1, :], weight)
    rank = mul(listed.astype(LOW), low_if(before))
    diagonal = number(square, 0) == number(square, 1)
    bounds = jnp.where(diagonal, limits_ref[...].astype(WIDE), 0.0)
    kept = (listed > 0.0) & (rank < jnp.sum(bounds, axis=1, keepdims=True))
    rank = jnp.where(kept, rank, -1.0)
    rank_out[...] = rank
    weight_out[...] = weight
    spread = mul(owner, rank.astype(LOW))
    tokens = tokens_ref[...]
    lanes = tokens.shape[1] // 2
    picked = jnp.concatenate([low_if(spread == left), low_if(spread == right)], axis=1)
    sides = jnp.concatenate([tokens[:, :lanes], tokens[:, lanes:]], axis=0)
    tok_out[...] = mul(picked, sides).reshape(experts, chunk, lanes).astype(LOW)


def grad_kernel(pad, rank_ref, weight_ref, clip_ref, cot_ref, cot_out):
    experts, tok_rows = rank_ref.shape
    chunk = 2 * pad
    slots = experts * chunk
    owner = owners((slots, experts), 0, chunk)
    left, right = wanted((slots, tok_rows), 0, pad)
    spread = mul(owner, rank_ref[...].astype(LOW))
    high, rest = split_low(weight_ref[...] * clip_ref[...].astype(WIDE))
    high, rest = mul(owner, high), mul(owner, rest)
    coefs = jnp.concatenate(
        [
            jnp.where(spread == place, part, 0.0).astype(LOW)
            for part in (high, rest)
            for place in (left, right)
        ],
        axis=1,
    )
    cot = cot_ref[...]
    lanes = cot.shape[1] // 2
    sides = jnp.concatenate([cot[:, :lanes], cot[:, lanes:]] * 2, axis=0)
    cot_out[...] = mul(coefs, sides).reshape(experts, chunk, lanes).astype(LOW)


def table_kernel(pad, rank_ref, weight_ref, pick_out, weight_out):
    experts, tok_rows = rank_ref.shape
    chunk = 2 * pad
    slots = experts * chunk
    owner = owners((experts, slots), 1, chunk)
    spread = mul(rank_ref[...].T.astype(LOW), owner)
    high, rest = split_low(weight_ref[...].T)
    high, rest = mul(high, owner), mul(rest, owner)
    for side, place in enumerate(wanted((tok_rows, slots), 1, pad)):
        picked = spread == place
        pick_out[side * tok_rows : (side + 1) * tok_rows, :] = low_if(picked)
        for at, part in enumerate((high, rest)):
            first = (2 * side + at) * tok_rows
            weight_out[first : first + tok_rows, :] = jnp.where(picked, part, 0.0).astype(LOW)


def combine_kernel(parts, table_ref, rows_ref, out_ref):
    tok_rows, width = out_ref.shape
    lanes = width // 2
    sums = mul(table_ref[...], rows_ref[...].reshape(table_ref.shape[1], lanes))
    for side in range(2):
        total = sums[parts * side * tok_rows : (parts * side + 1) * tok_rows]
        for at in range(1, parts):
            first = (parts * side + at) * tok_rows
            total = total + sums[first : first + tok_rows]
        out_ref[:, side * lanes : (side + 1) * lanes] = total.astype(LOW)


def shifts(shape, row_axis, capacity, pad, side):
    row = number(shape, row_axis)
    block = jnp.floor((row + 0.5) * (1.0 / capacity))
    return low_if(
        number(shape, 1 - row_axis) == row + (2 * pad - capacity) * block + pad * side
    )


GROUP = 8


def unpack_kernel(capacity, pad, core_ref, chunks_ref, keep_out, give_out):
    lanes = chunks_ref.shape[2]
    half = chunks_ref.shape[0] // 2
    rows, slots = GROUP * capacity, GROUP * 2 * pad
    moves = [shifts((rows, slots), 0, capacity, pad, side) for side in range(2)]
    core = core_ref[0]
    for out_ref, base in ((keep_out, core * half), (give_out, (1 - core) * half)):
        for at in range(half // GROUP):
            chunk = chunks_ref[pl.ds(base + at * GROUP, GROUP)].reshape(slots, lanes)
            for side in range(2):
                out_ref[at * rows : (at + 1) * rows, side * lanes : (side + 1) * lanes] = mul(
                    moves[side], chunk
                ).astype(LOW)


def pack_kernel(capacity, pad, core_ref, mine_ref, got_ref, chunks_out):
    lanes = chunks_out.shape[2]
    half = chunks_out.shape[0] // 2
    rows, slots = GROUP * capacity, GROUP * 2 * pad
    moves = [shifts((slots, rows), 1, capacity, pad, side) for side in range(2)]
    core = core_ref[0]
    for in_ref, base in ((mine_ref, core * half), (got_ref, (1 - core) * half)):
        for at in range(half // GROUP):
            block = in_ref[at * rows : (at + 1) * rows, :]
            chunk = mul(moves[0], block[:, :lanes]) + mul(moves[1], block[:, lanes:])
            chunks_out[pl.ds(base + at * GROUP, GROUP)] = chunk.reshape(
                GROUP, 2 * pad, lanes
            ).astype(LOW)


def gate_up_kernel(keep_ref, got_ref, gate_ref, up_ref, other_ref, out_ref):
    ff = gate_ref.shape[1]
    keep, got = keep_ref[...], got_ref[...]
    for at, own_ref in enumerate((gate_ref, up_ref)):
        cols = slice(at * ff, (at + 1) * ff)
        out_ref[:, cols] = (mul(keep, own_ref[...]) + mul(got, other_ref[:, cols])).astype(LOW)


def body(
    tokens, routes, combine, clip_mask, limits, cotangent, gate_weight, up_weight, down_weight
):
    tok_rows, top_count = routes.shape
    experts = limits.shape[0]
    capacity = 9 * tok_rows * top_count // (8 * experts)
    pad = -(-capacity // 4) * 4
    half = experts * capacity // 2
    width = tokens.shape[1]
    lanes = width // 2
    slots = experts * 2 * pad
    ff = gate_weight.shape[2]
    devices = lax.axis_size("dp")
    chips = devices // 2
    core = (lax.axis_index("dp") % 2).astype(jnp.int32).reshape(1)
    column = [[2 * chip + which for chip in range(chips)] for which in range(2)]
    swap_pairs = [(device, device ^ 1) for device in range(devices)]
    chunk_shape = jax.ShapeDtypeStruct((experts, 2 * pad, lanes), LOW)
    rank_shape = jax.ShapeDtypeStruct((experts, tok_rows), WIDE)
    half_shape = jax.ShapeDtypeStruct((half, width), LOW)
    tok_shape = jax.ShapeDtypeStruct((tok_rows, width), LOW)
    in_smem = pl.BlockSpec(memory_space=pltpu.SMEM)
    in_vmem = pl.BlockSpec(memory_space=pltpu.VMEM)
    anywhere = pl.BlockSpec(memory_space=pl.ANY)
    params = pltpu.CompilerParams(vmem_limit_bytes=40 * 1024 * 1024)

    def swap(values):
        return lax.ppermute(values, "dp", swap_pairs)

    def exchange(chunks):
        return lax.all_to_all(chunks, "expert", split_axis=0, concat_axis=0, tiled=True)

    def unpack(chunks):
        keep, give = pl.pallas_call(
            functools.partial(unpack_kernel, capacity, pad),
            out_shape=(half_shape, half_shape),
            in_specs=[in_smem, in_vmem],
            compiler_params=params,
            name="unpack",
        )(core, chunks)
        return keep, swap(give)

    def pack(mine, got):
        return pl.pallas_call(
            functools.partial(pack_kernel, capacity, pad),
            out_shape=chunk_shape,
            in_specs=[in_smem, in_vmem, in_vmem],
            compiler_params=params,
            name="pack",
        )(core, mine, got)

    def merge(parts, table, chunks):
        return pl.pallas_call(
            functools.partial(combine_kernel, parts),
            out_shape=tok_shape,
            compiler_params=params,
            name="merge",
        )(table, chunks)

    gate_own, up_own, down_own = gate_weight[0], up_weight[0], down_weight[0]
    gu_own = jnp.concatenate([gate_own, up_own], axis=1)
    gu_other = swap(gu_own)
    down_other = swap(down_own)

    token_send, rank, weight = pl.pallas_call(
        functools.partial(token_kernel, pad),
        out_shape=(chunk_shape, rank_shape, rank_shape),
        in_specs=[anywhere] * 4,
        scratch_shapes=[
            pltpu.VMEM((top_count, tok_rows), jnp.int32),
            pltpu.VMEM((top_count, tok_rows), WIDE),
            pltpu.VMEM((1, experts), jnp.int32),
            pltpu.VMEM((tok_rows, width), LOW),
            pltpu.SemaphoreType.DMA((4,)),
        ],
        compiler_params=params,
        name="token_rows",
    )(routes.T, combine.T, limits.reshape(1, experts), tokens)
    token_keep, token_got = unpack(exchange(token_send))
    gate_up = pl.pallas_call(
        gate_up_kernel,
        out_shape=jax.ShapeDtypeStruct((half, 2 * ff), LOW),
        compiler_params=params,
        name="gate_up",
    )(token_keep, token_got, gate_own, up_own, gu_other)
    shares = lax.psum_scatter(
        gate_up, "dp", scatter_dimension=0, tiled=True, axis_index_groups=column
    ).astype(WIDE)
    grad_send = pl.pallas_call(
        functools.partial(grad_kernel, pad),
        out_shape=chunk_shape,
        compiler_params=params,
        name="grad_rows",
    )(rank, weight, clip_mask.reshape(1, tok_rows), cotangent)
    grad_keep, grad_got = unpack(exchange(grad_send))
    grad_part = (
        (against(grad_keep, down_own) + against(grad_got, down_other))
        .astype(LOW)
        .reshape(chips, half // chips, ff)
    )
    grad_hidden = jnp.sum(
        lax.all_to_all(
            grad_part, "dp", split_axis=0, concat_axis=0, tiled=True, axis_index_groups=column
        ).astype(WIDE),
        axis=0,
    )
    gate_val, up_val = shares[:, :ff], shares[:, ff:]
    active, slope = swish_parts(gate_val)
    hidden = (active * up_val).astype(LOW)
    derived = jnp.concatenate(
        [(grad_hidden * up_val * slope).astype(LOW), (grad_hidden * active).astype(LOW)], axis=1
    )
    derived_full = lax.all_gather(derived, "dp", axis=0, tiled=True, axis_index_groups=column)
    hidden_full = lax.all_gather(hidden, "dp", axis=0, tiled=True, axis_index_groups=column)
    out_got = swap(mul(hidden_full, down_other).astype(LOW))
    back_rows = exchange(pack(mul(hidden_full, down_own).astype(LOW), out_got))
    input_got = swap(against(derived_full, gu_other).astype(LOW))
    grads_back = exchange(pack(against(derived_full, gu_own).astype(LOW), input_got))

    lower_got = swap(outer(hidden_full, grad_got).astype(LOW))
    down_grads = (outer(hidden_full, grad_keep) + lower_got.astype(WIDE)).astype(LOW)
    upper_got = swap(outer(token_got, derived_full).astype(LOW)).astype(WIDE)
    gate_grads = (outer(token_keep, derived_full[:, :ff]) + upper_got[:, :ff]).astype(LOW)
    up_grads = (outer(token_keep, derived_full[:, ff:]) + upper_got[:, ff:]).astype(LOW)

    picks, weights = pl.pallas_call(
        functools.partial(table_kernel, pad),
        out_shape=(
            jax.ShapeDtypeStruct((2 * tok_rows, slots), LOW),
            jax.ShapeDtypeStruct((4 * tok_rows, slots), LOW),
        ),
        compiler_params=params,
        name="tables",
    )(rank, weight)
    layer_out = merge(2, weights, back_rows)
    token_grads = merge(1, picks, grads_back)
    return (layer_out, token_grads, gate_grads[None], up_grads[None], down_grads[None])


def solution(mesh):
    in_specs = (
        P("expert", "dp"),
        P("expert", None),
        P("expert", None),
        P("expert"),
        P(),
        P("expert", "dp"),
        P("expert", "dp", None),
        P("expert", "dp", None),
        P("expert", None, "dp"),
    )
    out_specs = (
        P("expert", "dp"),
        P("expert", "dp"),
        P("expert", "dp", None),
        P("expert", "dp", None),
        P("expert", None, "dp"),
    )
    return jax.shard_map(body, mesh=mesh, in_specs=in_specs, out_specs=out_specs, check_vma=False)
```

```python
import functools

import jax
import jax.numpy as jnp
from jax import lax
from jax.experimental import pallas as pl
from jax.experimental.pallas import tpu as pltpu
from jax.sharding import PartitionSpec as P

LOW = jnp.bfloat16
WIDE = jnp.float32


def swish_parts(gate_val):
    sigma = jax.nn.sigmoid(gate_val)
    return (gate_val * sigma, sigma * (1.0 + gate_val * (1.0 - sigma)))


def mul(left, right):
    return jnp.dot(left, right, preferred_element_type=WIDE)


def split_low(values):
    high = values.astype(LOW)
    return high, (values - high.astype(WIDE)).astype(LOW)


def outer(left, right):
    return lax.dot_general(left, right, (((0,), (0,)), ((), ())), preferred_element_type=WIDE)


def against(left, right):
    return lax.dot_general(left, right, (((1,), (1,)), ((), ())), preferred_element_type=WIDE)


def number(shape, axis):
    return lax.broadcasted_iota(jnp.int32, shape, axis).astype(WIDE)


def low_if(condition):
    return jnp.where(condition, 1.0, 0.0).astype(LOW)


def remainder(values, step):
    return values - step * jnp.floor((values + 0.5) * (1.0 / step))


def owners(shape, slot_axis, chunk):
    offset = number(shape, slot_axis) - chunk * number(shape, 1 - slot_axis)
    return low_if((offset >= 0.0) & (offset < chunk))


def wanted(shape, slot_axis, pad):
    within = remainder(number(shape, slot_axis), 2 * pad)
    left = jnp.where(within < pad, within, -5.0)
    right = jnp.where(within >= pad, within - pad, -5.0)
    return left, right


def token_kernel(
    pad,
    routes_hbm,
    combine_hbm,
    limits_hbm,
    tokens_hbm,
    tok_out,
    rank_out,
    weight_out,
    routes_ref,
    combine_ref,
    limits_ref,
    tokens_ref,
    sems,
):
    copies = [
        pltpu.make_async_copy(source, target, sems.at[at])
        for at, (source, target) in enumerate(
            (
                (routes_hbm, routes_ref),
                (combine_hbm, combine_ref),
                (limits_hbm, limits_ref),
                (tokens_hbm, tokens_ref),
            )
        )
    ]
    for copy in copies:
        copy.start()
    top_count, tok_rows = routes_ref.shape
    experts = limits_ref.shape[1]
    chunk = 2 * pad
    slots = experts * chunk
    owner = owners((slots, experts), 0, chunk)
    left, right = wanted((slots, tok_rows), 0, pad)
    before = number((tok_rows, tok_rows), 0) < number((tok_rows, tok_rows), 1)
    square = (experts, experts)
    for copy in copies:
        copy.wait()
    labels = lax.broadcasted_iota(jnp.int32, (experts, tok_rows), 0)
    listed = jnp.zeros((experts, tok_rows), WIDE)
    weight = jnp.zeros((experts, tok_rows), WIDE)
    for entry in range(top_count):
        match = routes_ref[entry : entry + 1, :] == labels
        listed = jnp.where(match, 1.0, listed)
        weight = jnp.where(match, combine_ref[entry : entry + 1, :], weight)
    rank = mul(listed.astype(LOW), low_if(before))
    diagonal = number(square, 0) == number(square, 1)
    bounds = jnp.where(diagonal, limits_ref[...].astype(WIDE), 0.0)
    kept = (listed > 0.0) & (rank < jnp.sum(bounds, axis=1, keepdims=True))
    rank = jnp.where(kept, rank, -1.0)
    rank_out[...] = rank
    weight_out[...] = weight
    spread = mul(owner, rank.astype(LOW))
    tokens = tokens_ref[...]
    lanes = tokens.shape[1] // 2
    picked = jnp.concatenate([low_if(spread == left), low_if(spread == right)], axis=1)
    sides = jnp.concatenate([tokens[:, :lanes], tokens[:, lanes:]], axis=0)
    tok_out[...] = mul(picked, sides).reshape(experts, chunk, lanes).astype(LOW)


def grad_kernel(pad, rank_ref, weight_ref, clip_ref, cot_ref, cot_out):
    experts, tok_rows = rank_ref.shape
    chunk = 2 * pad
    slots = experts * chunk
    owner = owners((slots, experts), 0, chunk)
    left, right = wanted((slots, tok_rows), 0, pad)
    spread = mul(owner, rank_ref[...].astype(LOW))
    high, rest = split_low(weight_ref[...] * clip_ref[...].astype(WIDE))
    high, rest = mul(owner, high), mul(owner, rest)
    coefs = jnp.concatenate(
        [
            jnp.where(spread == place, part, 0.0).astype(LOW)
            for part in (high, rest)
            for place in (left, right)
        ],
        axis=1,
    )
    cot = cot_ref[...]
    lanes = cot.shape[1] // 2
    sides = jnp.concatenate([cot[:, :lanes], cot[:, lanes:]] * 2, axis=0)
    cot_out[...] = mul(coefs, sides).reshape(experts, chunk, lanes).astype(LOW)


def table_kernel(pad, rank_ref, weight_ref, pick_out, weight_out):
    experts, tok_rows = rank_ref.shape
    chunk = 2 * pad
    slots = experts * chunk
    owner = owners((experts, slots), 1, chunk)
    spread = mul(rank_ref[...].T.astype(LOW), owner)
    high, rest = split_low(weight_ref[...].T)
    high, rest = mul(high, owner), mul(rest, owner)
    for side, place in enumerate(wanted((tok_rows, slots), 1, pad)):
        picked = spread == place
        pick_out[side * tok_rows : (side + 1) * tok_rows, :] = low_if(picked)
        for at, part in enumerate((high, rest)):
            first = (2 * side + at) * tok_rows
            weight_out[first : first + tok_rows, :] = jnp.where(picked, part, 0.0).astype(LOW)


def combine_kernel(parts, table_ref, rows_ref, out_ref):
    tok_rows, width = out_ref.shape
    lanes = width // 2
    sums = mul(table_ref[...], rows_ref[...].reshape(table_ref.shape[1], lanes))
    for side in range(2):
        total = sums[parts * side * tok_rows : (parts * side + 1) * tok_rows]
        for at in range(1, parts):
            first = (parts * side + at) * tok_rows
            total = total + sums[first : first + tok_rows]
        out_ref[:, side * lanes : (side + 1) * lanes] = total.astype(LOW)


def shifts(shape, row_axis, capacity, pad, side):
    row = number(shape, row_axis)
    block = jnp.floor((row + 0.5) * (1.0 / capacity))
    return low_if(
        number(shape, 1 - row_axis) == row + (2 * pad - capacity) * block + pad * side
    )


GROUP = 8


def unpack_kernel(capacity, pad, core_ref, chunks_ref, keep_out, give_out):
    lanes = chunks_ref.shape[2]
    half = chunks_ref.shape[0] // 2
    rows, slots = GROUP * capacity, GROUP * 2 * pad
    moves = [shifts((rows, slots), 0, capacity, pad, side) for side in range(2)]
    core = core_ref[0]
    for out_ref, base in ((keep_out, core * half), (give_out, (1 - core) * half)):
        for at in range(half // GROUP):
            chunk = chunks_ref[pl.ds(base + at * GROUP, GROUP)].reshape(slots, lanes)
            for side in range(2):
                out_ref[at * rows : (at + 1) * rows, side * lanes : (side + 1) * lanes] = mul(
                    moves[side], chunk
                ).astype(LOW)


def pack_kernel(capacity, pad, core_ref, mine_ref, got_ref, chunks_out):
    lanes = chunks_out.shape[2]
    half = chunks_out.shape[0] // 2
    rows, slots = GROUP * capacity, GROUP * 2 * pad
    moves = [shifts((slots, rows), 1, capacity, pad, side) for side in range(2)]
    core = core_ref[0]
    for in_ref, base in ((mine_ref, core * half), (got_ref, (1 - core) * half)):
        for at in range(half // GROUP):
            block = in_ref[at * rows : (at + 1) * rows, :]
            chunk = mul(moves[0], block[:, :lanes]) + mul(moves[1], block[:, lanes:])
            chunks_out[pl.ds(base + at * GROUP, GROUP)] = chunk.reshape(
                GROUP, 2 * pad, lanes
            ).astype(LOW)


def gate_up_kernel(keep_ref, got_ref, gate_ref, up_ref, other_ref, out_ref):
    ff = gate_ref.shape[1]
    keep, got = keep_ref[...], got_ref[...]
    for at, own_ref in enumerate((gate_ref, up_ref)):
        cols = slice(at * ff, (at + 1) * ff)
        out_ref[:, cols] = (mul(keep, own_ref[...]) + mul(got, other_ref[:, cols])).astype(LOW)


def hidden_grad_kernel(parity_ref, keep_ref, got_ref, own_ref, other_ref, stay_out, leave_out):
    block = stay_out.shape[1]
    parts = against(keep_ref[...], own_ref[...]) + against(got_ref[...], other_ref[...])
    odd = parity_ref[0] == 1
    for at in range(stay_out.shape[0]):
        first = parts[2 * at * block : (2 * at + 1) * block]
        second = parts[(2 * at + 1) * block : (2 * at + 2) * block]
        stay_out[at] = jnp.where(odd, second, first).astype(LOW)
        leave_out[at] = jnp.where(odd, first, second).astype(LOW)


def body(
    tokens, routes, combine, clip_mask, limits, cotangent, gate_weight, up_weight, down_weight
):
    tok_rows, top_count = routes.shape
    experts = limits.shape[0]
    capacity = 9 * tok_rows * top_count // (8 * experts)
    pad = -(-capacity // 4) * 4
    half = experts * capacity // 2
    width = tokens.shape[1]
    lanes = width // 2
    slots = experts * 2 * pad
    ff = gate_weight.shape[2]
    devices = lax.axis_size("dp")
    chips = devices // 2
    spot = lax.axis_index("dp").astype(jnp.int32)
    core = (spot % 2).reshape(1)
    parity = (spot // 2 % 2).reshape(1)
    column = [[2 * chip + which for chip in range(chips)] for which in range(2)]
    swap_pairs = [(device, device ^ 1) for device in range(devices)]
    near_pairs = []
    for chip in range(chips):
        near_pairs.append((2 * chip, 2 * (chip ^ 1)))
        near_pairs.append((2 * chip + 1, 2 * ((((chip - 1) ^ 1) + 1) % chips) + 1))
    alike = [
        [2 * chip + which for chip in range(first, chips, 2)] for which in range(2) for first in range(2)
    ]
    chunk_shape = jax.ShapeDtypeStruct((experts, 2 * pad, lanes), LOW)
    rank_shape = jax.ShapeDtypeStruct((experts, tok_rows), WIDE)
    half_shape = jax.ShapeDtypeStruct((half, width), LOW)
    tok_shape = jax.ShapeDtypeStruct((tok_rows, width), LOW)
    in_smem = pl.BlockSpec(memory_space=pltpu.SMEM)
    in_vmem = pl.BlockSpec(memory_space=pltpu.VMEM)
    anywhere = pl.BlockSpec(memory_space=pl.ANY)
    params = pltpu.CompilerParams(vmem_limit_bytes=40 * 1024 * 1024)

    def swap(values):
        return lax.ppermute(values, "dp", swap_pairs)

    def exchange(chunks):
        return lax.all_to_all(chunks, "expert", split_axis=0, concat_axis=0, tiled=True)

    def unpack(chunks):
        keep, give = pl.pallas_call(
            functools.partial(unpack_kernel, capacity, pad),
            out_shape=(half_shape, half_shape),
            in_specs=[in_smem, in_vmem],
            compiler_params=params,
            name="unpack",
        )(core, chunks)
        return keep, swap(give)

    def pack(mine, got):
        return pl.pallas_call(
            functools.partial(pack_kernel, capacity, pad),
            out_shape=chunk_shape,
            in_specs=[in_smem, in_vmem, in_vmem],
            compiler_params=params,
            name="pack",
        )(core, mine, got)

    def merge(parts, table, chunks):
        return pl.pallas_call(
            functools.partial(combine_kernel, parts),
            out_shape=tok_shape,
            compiler_params=params,
            name="merge",
        )(table, chunks)

    gate_own, up_own, down_own = gate_weight[0], up_weight[0], down_weight[0]
    gu_own = jnp.concatenate([gate_own, up_own], axis=1)
    gu_other = swap(gu_own)
    down_other = swap(down_own)

    token_send, rank, weight = pl.pallas_call(
        functools.partial(token_kernel, pad),
        out_shape=(chunk_shape, rank_shape, rank_shape),
        in_specs=[anywhere] * 4,
        scratch_shapes=[
            pltpu.VMEM((top_count, tok_rows), jnp.int32),
            pltpu.VMEM((top_count, tok_rows), WIDE),
            pltpu.VMEM((1, experts), jnp.int32),
            pltpu.VMEM((tok_rows, width), LOW),
            pltpu.SemaphoreType.DMA((4,)),
        ],
        compiler_params=pltpu.CompilerParams(vmem_limit_bytes=63 * 1024 * 1024),
        name="token_rows",
    )(routes.T, combine.T, limits.reshape(1, experts), tokens)
    token_keep, token_got = unpack(exchange(token_send))
    gate_up = pl.pallas_call(
        gate_up_kernel,
        out_shape=jax.ShapeDtypeStruct((half, 2 * ff), LOW),
        compiler_params=params,
        name="gate_up",
    )(token_keep, token_got, gate_own, up_own, gu_other)
    grad_send = pl.pallas_call(
        functools.partial(grad_kernel, pad),
        out_shape=chunk_shape,
        compiler_params=params,
        name="grad_rows",
    )(rank, weight, clip_mask.reshape(1, tok_rows), cotangent)
    gate_up, grad_send = lax.optimization_barrier((gate_up, grad_send))
    shares = lax.psum_scatter(
        gate_up, "dp", scatter_dimension=0, tiled=True, axis_index_groups=column
    ).astype(WIDE)
    grad_keep, grad_got = unpack(exchange(grad_send))
    part_shape = jax.ShapeDtypeStruct((chips // 2, half // chips, ff), LOW)
    stay, leave = pl.pallas_call(
        hidden_grad_kernel,
        out_shape=(part_shape, part_shape),
        in_specs=[in_smem] + [in_vmem] * 4,
        compiler_params=params,
        name="hidden_grad",
    )(parity, grad_keep, grad_got, down_own, down_other)
    joined = (stay.astype(WIDE) + lax.ppermute(leave, "dp", near_pairs).astype(WIDE)).astype(LOW)
    grad_hidden = jnp.sum(
        lax.all_to_all(
            joined, "dp", split_axis=0, concat_axis=0, tiled=True, axis_index_groups=alike
        ).astype(WIDE),
        axis=0,
    )
    gate_val, up_val = shares[:, :ff], shares[:, ff:]
    active, slope = swish_parts(gate_val)
    hidden = (active * up_val).astype(LOW)
    derived = jnp.concatenate(
        [(grad_hidden * up_val * slope).astype(LOW), (grad_hidden * active).astype(LOW)], axis=1
    )
    derived_full = lax.all_gather(derived, "dp", axis=0, tiled=True, axis_index_groups=column)
    hidden_full = lax.all_gather(hidden, "dp", axis=0, tiled=True, axis_index_groups=column)
    out_got = swap(mul(hidden_full, down_other).astype(LOW))
    back_rows = exchange(pack(mul(hidden_full, down_own).astype(LOW), out_got))
    input_got = swap(against(derived_full, gu_other).astype(LOW))
    grads_back = exchange(pack(against(derived_full, gu_own).astype(LOW), input_got))

    lower_got = swap(outer(hidden_full, grad_got).astype(LOW))
    down_grads = (outer(hidden_full, grad_keep) + lower_got.astype(WIDE)).astype(LOW)
    upper_got = swap(outer(token_got, derived_full).astype(LOW)).astype(WIDE)
    gate_grads = (outer(token_keep, derived_full[:, :ff]) + upper_got[:, :ff]).astype(LOW)
    up_grads = (outer(token_keep, derived_full[:, ff:]) + upper_got[:, ff:]).astype(LOW)

    picks, weights = pl.pallas_call(
        functools.partial(table_kernel, pad),
        out_shape=(
            jax.ShapeDtypeStruct((2 * tok_rows, slots), LOW),
            jax.ShapeDtypeStruct((4 * tok_rows, slots), LOW),
        ),
        compiler_params=params,
        name="tables",
    )(rank, weight)
    layer_out = merge(2, weights, back_rows)
    token_grads = merge(1, picks, grads_back)
    return (layer_out, token_grads, gate_grads[None], up_grads[None], down_grads[None])


def solution(mesh):
    in_specs = (
        P("expert", "dp"),
        P("expert", None),
        P("expert", None),
        P("expert"),
        P(),
        P("expert", "dp"),
        P("expert", "dp", None),
        P("expert", "dp", None),
        P("expert", None, "dp"),
    )
    out_specs = (
        P("expert", "dp"),
        P("expert", "dp"),
        P("expert", "dp", None),
        P("expert", "dp", None),
        P("expert", None, "dp"),
    )
    return jax.shard_map(body, mesh=mesh, in_specs=in_specs, out_specs=out_specs, check_vma=False)
```

```python
import functools

import jax
import jax.numpy as jnp
from jax import lax
from jax.experimental import pallas as pl
from jax.experimental.pallas import tpu as pltpu
from jax.sharding import PartitionSpec as P

LOW = jnp.bfloat16
WIDE = jnp.float32


def swish_parts(gate_val):
    sigma = jax.nn.sigmoid(gate_val)
    return (gate_val * sigma, sigma * (1.0 + gate_val * (1.0 - sigma)))


def mul(left, right):
    return jnp.dot(left, right, preferred_element_type=WIDE)


def split_low(values):
    high = values.astype(LOW)
    return high, (values - high.astype(WIDE)).astype(LOW)


def outer(left, right):
    return lax.dot_general(left, right, (((0,), (0,)), ((), ())), preferred_element_type=WIDE)


def against(left, right):
    return lax.dot_general(left, right, (((1,), (1,)), ((), ())), preferred_element_type=WIDE)


def number(shape, axis):
    return lax.broadcasted_iota(jnp.int32, shape, axis).astype(WIDE)


def low_if(condition):
    return jnp.where(condition, 1.0, 0.0).astype(LOW)


def remainder(values, step):
    return values - step * jnp.floor((values + 0.5) * (1.0 / step))


def owners(shape, slot_axis, chunk):
    offset = number(shape, slot_axis) - chunk * number(shape, 1 - slot_axis)
    return low_if((offset >= 0.0) & (offset < chunk))


def wanted(shape, slot_axis, pad):
    within = remainder(number(shape, slot_axis), 2 * pad)
    left = jnp.where(within < pad, within, -5.0)
    right = jnp.where(within >= pad, within - pad, -5.0)
    return left, right


def places(group, capacity, transposed):
    size = 4 * group * capacity
    chunked = number((1, size) if transposed else (size, 1), 1 if transposed else 0)
    expert = jnp.floor((chunked + 0.5) * (1.0 / (4 * capacity)))
    within = chunked - 4 * capacity * expert
    piece = jnp.floor((within + 0.5) * (1.0 / capacity))
    stacked = within - capacity * piece + capacity * (expert + group * piece)
    return low_if(number((size, size), 0 if transposed else 1) == stacked)


GROUP = 8


def dispatch_kernel(
    capacity,
    routes_hbm,
    combine_hbm,
    clip_hbm,
    limits_hbm,
    tokens_hbm,
    cot_hbm,
    chunks_out,
    rank_out,
    weight_out,
    routes_ref,
    combine_ref,
    clip_ref,
    limits_ref,
    tokens_ref,
    cot_ref,
    sems,
):
    copies = [
        pltpu.make_async_copy(source, target, sems.at[at])
        for at, (source, target) in enumerate(
            (
                (routes_hbm, routes_ref),
                (combine_hbm, combine_ref),
                (clip_hbm, clip_ref),
                (limits_hbm, limits_ref),
                (tokens_hbm, tokens_ref),
                (cot_hbm, cot_ref),
            )
        )
    ]
    for copy in copies:
        copy.start()
    top_count, tok_rows = routes_ref.shape
    experts = limits_ref.shape[1]
    slots = experts * capacity
    owner = owners((slots, experts), 0, capacity)
    place = remainder(number((slots, 1), 0), capacity)
    before = number((tok_rows, tok_rows), 0) < number((tok_rows, tok_rows), 1)
    square = (experts, experts)
    for copy in copies:
        copy.wait()
    labels = lax.broadcasted_iota(jnp.int32, (experts, tok_rows), 0)
    listed = jnp.zeros((experts, tok_rows), WIDE)
    weight = jnp.zeros((experts, tok_rows), WIDE)
    for entry in range(top_count):
        match = routes_ref[entry : entry + 1, :] == labels
        listed = jnp.where(match, 1.0, listed)
        weight = jnp.where(match, combine_ref[entry : entry + 1, :], weight)
    rank = mul(listed.astype(LOW), low_if(before))
    diagonal = number(square, 0) == number(square, 1)
    bounds = jnp.where(diagonal, limits_ref[...].astype(WIDE), 0.0)
    kept = (listed > 0.0) & (rank < jnp.sum(bounds, axis=1, keepdims=True))
    rank = jnp.where(kept, rank, -1.0)
    rank_out[...] = rank
    weight_out[...] = weight
    picked = mul(owner, rank.astype(LOW)) == place
    tok_rows_all = mul(low_if(picked), tokens_ref[...]).astype(LOW)
    coefs = jnp.concatenate(
        [
            jnp.where(picked, mul(owner, part), 0.0).astype(LOW)
            for part in split_low(weight * clip_ref[...].astype(WIDE))
        ],
        axis=1,
    )
    cot = cot_ref[...]
    cot_rows_all = mul(coefs, jnp.concatenate([cot, cot], axis=0)).astype(LOW)
    lanes = cot.shape[1] // 2
    moves = places(GROUP, capacity, False)
    rows = GROUP * capacity
    for at in range(experts // GROUP):
        block = slice(at * rows, (at + 1) * rows)
        stacked = jnp.concatenate(
            [
                part[block, side * lanes : (side + 1) * lanes]
                for part in (tok_rows_all, cot_rows_all)
                for side in range(2)
            ],
            axis=0,
        )
        chunks_out[at * GROUP : (at + 1) * GROUP] = (
            mul(moves, stacked).reshape(GROUP, 4 * capacity, lanes).astype(LOW)
        )


def table_kernel(pad, rank_ref, weight_ref, pick_out, weight_out):
    experts, tok_rows = rank_ref.shape
    chunk = 2 * pad
    slots = experts * chunk
    owner = owners((experts, slots), 1, chunk)
    spread = mul(rank_ref[...].T.astype(LOW), owner)
    high, rest = split_low(weight_ref[...].T)
    high, rest = mul(high, owner), mul(rest, owner)
    for side, place in enumerate(wanted((tok_rows, slots), 1, pad)):
        picked = spread == place
        pick_out[side * tok_rows : (side + 1) * tok_rows, :] = low_if(picked)
        for at, part in enumerate((high, rest)):
            first = (2 * side + at) * tok_rows
            weight_out[first : first + tok_rows, :] = jnp.where(picked, part, 0.0).astype(LOW)


def combine_kernel(parts, table_ref, rows_ref, out_ref):
    tok_rows, width = out_ref.shape
    lanes = width // 2
    sums = mul(table_ref[...], rows_ref[...].reshape(table_ref.shape[1], lanes))
    for side in range(2):
        total = sums[parts * side * tok_rows : (parts * side + 1) * tok_rows]
        for at in range(1, parts):
            first = (parts * side + at) * tok_rows
            total = total + sums[first : first + tok_rows]
        out_ref[:, side * lanes : (side + 1) * lanes] = total.astype(LOW)


def shifts(shape, row_axis, capacity, pad, side):
    row = number(shape, row_axis)
    block = jnp.floor((row + 0.5) * (1.0 / capacity))
    return low_if(
        number(shape, 1 - row_axis) == row + (2 * pad - capacity) * block + pad * side
    )


def unpack_kernel(capacity, core_ref, chunks_ref, tok_out, cot_out, give_out):
    lanes = chunks_ref.shape[2]
    half = chunks_ref.shape[0] // 2
    rows = GROUP * capacity
    moves = places(GROUP, capacity, True)
    core = core_ref[0]
    for (first_out, first), (second_out, second), base in (
        ((tok_out, 0), (cot_out, 0), core * half),
        ((give_out, 0), (give_out, half * capacity), (1 - core) * half),
    ):
        for at in range(half // GROUP):
            chunk = chunks_ref[pl.ds(base + at * GROUP, GROUP)].reshape(4 * rows, lanes)
            pieces = mul(moves, chunk).astype(LOW)
            for piece in range(4):
                out_ref, start = ((first_out, first), (second_out, second))[piece // 2]
                start = start + at * rows
                cols = slice(piece % 2 * lanes, (piece % 2 + 1) * lanes)
                out_ref[start : start + rows, cols] = pieces[piece * rows : (piece + 1) * rows]


def pack_kernel(capacity, pad, core_ref, mine_ref, got_ref, chunks_out):
    lanes = chunks_out.shape[2]
    half = chunks_out.shape[0] // 2
    rows, slots = GROUP * capacity, GROUP * 2 * pad
    moves = [shifts((slots, rows), 1, capacity, pad, side) for side in range(2)]
    core = core_ref[0]
    for in_ref, base in ((mine_ref, core * half), (got_ref, (1 - core) * half)):
        for at in range(half // GROUP):
            block = in_ref[at * rows : (at + 1) * rows, :]
            chunk = mul(moves[0], block[:, :lanes]) + mul(moves[1], block[:, lanes:])
            chunks_out[pl.ds(base + at * GROUP, GROUP)] = chunk.reshape(
                GROUP, 2 * pad, lanes
            ).astype(LOW)


def gate_up_kernel(keep_ref, got_ref, gate_ref, up_ref, other_ref, out_ref):
    half, ff = keep_ref.shape[0], gate_ref.shape[1]
    keep, got = keep_ref[...], got_ref[0:half, :]
    for at, own_ref in enumerate((gate_ref, up_ref)):
        cols = slice(at * ff, (at + 1) * ff)
        out_ref[:, cols] = (mul(keep, own_ref[...]) + mul(got, other_ref[:, cols])).astype(LOW)


def hidden_grad_kernel(keep_ref, got_ref, own_ref, other_ref, out_ref):
    half = keep_ref.shape[0]
    out_ref[...] = (
        against(keep_ref[...], own_ref[...]) + against(got_ref[half:, :], other_ref[...])
    ).astype(LOW)


def activate_kernel(shares_ref, parts_ref, hidden_out, derived_out):
    ff = hidden_out.shape[1]
    gate_val = shares_ref[:, :ff].astype(WIDE)
    up_val = shares_ref[:, ff:].astype(WIDE)
    grad_hidden = parts_ref[0].astype(WIDE)
    for at in range(1, parts_ref.shape[0]):
        grad_hidden = grad_hidden + parts_ref[at].astype(WIDE)
    active, slope = swish_parts(gate_val)
    hidden_out[...] = (active * up_val).astype(LOW)
    derived_out[:, :ff] = (grad_hidden * up_val * slope).astype(LOW)
    derived_out[:, ff:] = (grad_hidden * active).astype(LOW)


def body(
    tokens, routes, combine, clip_mask, limits, cotangent, gate_weight, up_weight, down_weight
):
    tok_rows, top_count = routes.shape
    experts = limits.shape[0]
    capacity = 9 * tok_rows * top_count // (8 * experts)
    pad = -(-capacity // 4) * 4
    half = experts * capacity // 2
    width = tokens.shape[1]
    lanes = width // 2
    slots = experts * 2 * pad
    ff = gate_weight.shape[2]
    devices = lax.axis_size("dp")
    chips = devices // 2
    core = (lax.axis_index("dp") % 2).astype(jnp.int32).reshape(1)
    column = [[2 * chip + which for chip in range(chips)] for which in range(2)]
    swap_pairs = [(device, device ^ 1) for device in range(devices)]
    chunk_shape = jax.ShapeDtypeStruct((experts, 2 * pad, lanes), LOW)
    rank_shape = jax.ShapeDtypeStruct((experts, tok_rows), WIDE)
    half_shape = jax.ShapeDtypeStruct((half, width), LOW)
    tok_shape = jax.ShapeDtypeStruct((tok_rows, width), LOW)
    in_smem = pl.BlockSpec(memory_space=pltpu.SMEM)
    in_vmem = pl.BlockSpec(memory_space=pltpu.VMEM)
    anywhere = pl.BlockSpec(memory_space=pl.ANY)
    params = pltpu.CompilerParams(vmem_limit_bytes=40 * 1024 * 1024)

    def swap(values):
        return lax.ppermute(values, "dp", swap_pairs)

    def exchange(chunks):
        return lax.all_to_all(chunks, "expert", split_axis=0, concat_axis=0, tiled=True)

    def pack(mine, got):
        return pl.pallas_call(
            functools.partial(pack_kernel, capacity, pad),
            out_shape=chunk_shape,
            in_specs=[in_smem, in_vmem, in_vmem],
            compiler_params=params,
            name="pack",
        )(core, mine, got)

    def merge(parts, table, chunks):
        return pl.pallas_call(
            functools.partial(combine_kernel, parts),
            out_shape=tok_shape,
            compiler_params=params,
            name="merge",
        )(table, chunks)

    gate_own, up_own, down_own = gate_weight[0], up_weight[0], down_weight[0]
    gu_own = jnp.concatenate([gate_own, up_own], axis=1)
    gu_other = swap(gu_own)
    down_other = swap(down_own)

    sent, rank, weight = pl.pallas_call(
        functools.partial(dispatch_kernel, capacity),
        out_shape=(
            jax.ShapeDtypeStruct((experts, 4 * capacity, lanes), LOW),
            rank_shape,
            rank_shape,
        ),
        in_specs=[anywhere] * 6,
        scratch_shapes=[
            pltpu.VMEM((top_count, tok_rows), jnp.int32),
            pltpu.VMEM((top_count, tok_rows), WIDE),
            pltpu.VMEM((1, tok_rows), jnp.int32),
            pltpu.VMEM((1, experts), jnp.int32),
            pltpu.VMEM((tok_rows, width), LOW),
            pltpu.VMEM((tok_rows, width), LOW),
            pltpu.SemaphoreType.DMA((6,)),
        ],
        compiler_params=pltpu.CompilerParams(vmem_limit_bytes=63 * 1024 * 1024),
        name="dispatch",
    )(
        routes.T,
        combine.T,
        clip_mask.reshape(1, tok_rows),
        limits.reshape(1, experts),
        tokens,
        cotangent,
    )
    token_keep, grad_keep, give = pl.pallas_call(
        functools.partial(unpack_kernel, capacity),
        out_shape=(half_shape, half_shape, jax.ShapeDtypeStruct((2 * half, width), LOW)),
        in_specs=[in_smem, in_vmem],
        compiler_params=params,
        name="unpack",
    )(core, exchange(sent))
    got = swap(give)
    token_got, grad_got = got[:half], got[half:]
    gate_up = pl.pallas_call(
        gate_up_kernel,
        out_shape=jax.ShapeDtypeStruct((half, 2 * ff), LOW),
        compiler_params=params,
        name="gate_up",
    )(token_keep, got, gate_own, up_own, gu_other)
    gate_up, grad_ready = lax.optimization_barrier((gate_up, grad_keep))
    shares = lax.psum_scatter(
        gate_up, "dp", scatter_dimension=0, tiled=True, axis_index_groups=column
    )
    grad_part = pl.pallas_call(
        hidden_grad_kernel,
        out_shape=jax.ShapeDtypeStruct((half, ff), LOW),
        compiler_params=params,
        name="hidden_grad",
    )(grad_ready, got, down_own, down_other)
    grad_parts = lax.all_to_all(
        grad_part.reshape(chips, half // chips, ff),
        "dp",
        split_axis=0,
        concat_axis=0,
        tiled=True,
        axis_index_groups=column,
    )
    hidden, derived = pl.pallas_call(
        activate_kernel,
        out_shape=(
            jax.ShapeDtypeStruct((half // chips, ff), LOW),
            jax.ShapeDtypeStruct((half // chips, 2 * ff), LOW),
        ),
        compiler_params=params,
        name="activate",
    )(shares, grad_parts)
    derived_full = lax.all_gather(derived, "dp", axis=0, tiled=True, axis_index_groups=column)
    hidden_full = lax.all_gather(hidden, "dp", axis=0, tiled=True, axis_index_groups=column)
    out_got = swap(mul(hidden_full, down_other).astype(LOW))
    back_rows = exchange(pack(mul(hidden_full, down_own).astype(LOW), out_got))
    input_got = swap(against(derived_full, gu_other).astype(LOW))
    grads_back = exchange(pack(against(derived_full, gu_own).astype(LOW), input_got))

    lower_got = swap(outer(hidden_full, grad_got).astype(LOW))
    down_grads = (outer(hidden_full, grad_keep) + lower_got.astype(WIDE)).astype(LOW)
    upper_got = swap(outer(token_got, derived_full).astype(LOW)).astype(WIDE)
    gate_grads = (outer(token_keep, derived_full[:, :ff]) + upper_got[:, :ff]).astype(LOW)
    up_grads = (outer(token_keep, derived_full[:, ff:]) + upper_got[:, ff:]).astype(LOW)

    picks, weights = pl.pallas_call(
        functools.partial(table_kernel, pad),
        out_shape=(
            jax.ShapeDtypeStruct((2 * tok_rows, slots), LOW),
            jax.ShapeDtypeStruct((4 * tok_rows, slots), LOW),
        ),
        compiler_params=params,
        name="tables",
    )(rank, weight)
    layer_out = merge(2, weights, back_rows)
    token_grads = merge(1, picks, grads_back)
    return (layer_out, token_grads, gate_grads[None], up_grads[None], down_grads[None])


def solution(mesh):
    in_specs = (
        P("expert", "dp"),
        P("expert", None),
        P("expert", None),
        P("expert"),
        P(),
        P("expert", "dp"),
        P("expert", "dp", None),
        P("expert", "dp", None),
        P("expert", None, "dp"),
    )
    out_specs = (
        P("expert", "dp"),
        P("expert", "dp"),
        P("expert", "dp", None),
        P("expert", "dp", None),
        P("expert", None, "dp"),
    )
    return jax.shard_map(body, mesh=mesh, in_specs=in_specs, out_specs=out_specs, check_vma=False)
```

```python
import functools

import jax
import jax.numpy as jnp
from jax import lax
from jax.experimental import pallas as pl
from jax.experimental.pallas import tpu as pltpu
from jax.sharding import PartitionSpec as P

LOW = jnp.bfloat16
WIDE = jnp.float32


def swish_parts(gate_val):
    sigma = jax.nn.sigmoid(gate_val)
    return (gate_val * sigma, sigma * (1.0 + gate_val * (1.0 - sigma)))


def mul(left, right):
    return jnp.dot(left, right, preferred_element_type=WIDE)


def split_low(values):
    high = values.astype(LOW)
    return high, (values - high.astype(WIDE)).astype(LOW)


def outer(left, right):
    return lax.dot_general(left, right, (((0,), (0,)), ((), ())), preferred_element_type=WIDE)


def against(left, right):
    return lax.dot_general(left, right, (((1,), (1,)), ((), ())), preferred_element_type=WIDE)


def number(shape, axis):
    return lax.broadcasted_iota(jnp.int32, shape, axis).astype(WIDE)


def low_if(condition):
    return jnp.where(condition, 1.0, 0.0).astype(LOW)


def remainder(values, step):
    return values - step * jnp.floor((values + 0.5) * (1.0 / step))


def owners(shape, slot_axis, chunk):
    offset = number(shape, slot_axis) - chunk * number(shape, 1 - slot_axis)
    return low_if((offset >= 0.0) & (offset < chunk))


def wanted(shape, slot_axis, pad):
    within = remainder(number(shape, slot_axis), 2 * pad)
    left = jnp.where(within < pad, within, -5.0)
    right = jnp.where(within >= pad, within - pad, -5.0)
    return left, right


def token_kernel(
    pad,
    routes_hbm,
    combine_hbm,
    limits_hbm,
    tokens_hbm,
    tok_out,
    rank_out,
    weight_out,
    routes_ref,
    combine_ref,
    limits_ref,
    tokens_ref,
    sems,
):
    copies = [
        pltpu.make_async_copy(source, target, sems.at[at])
        for at, (source, target) in enumerate(
            (
                (routes_hbm, routes_ref),
                (combine_hbm, combine_ref),
                (limits_hbm, limits_ref),
                (tokens_hbm, tokens_ref),
            )
        )
    ]
    for copy in copies:
        copy.start()
    top_count, tok_rows = routes_ref.shape
    experts = limits_ref.shape[1]
    chunk = 2 * pad
    slots = experts * chunk
    owner = owners((slots, experts), 0, chunk)
    left, right = wanted((slots, tok_rows), 0, pad)
    before = number((tok_rows, tok_rows), 0) < number((tok_rows, tok_rows), 1)
    square = (experts, experts)
    for copy in copies:
        copy.wait()
    labels = lax.broadcasted_iota(jnp.int32, (experts, tok_rows), 0)
    listed = jnp.zeros((experts, tok_rows), WIDE)
    weight = jnp.zeros((experts, tok_rows), WIDE)
    for entry in range(top_count):
        match = routes_ref[entry : entry + 1, :] == labels
        listed = jnp.where(match, 1.0, listed)
        weight = jnp.where(match, combine_ref[entry : entry + 1, :], weight)
    rank = mul(listed.astype(LOW), low_if(before))
    diagonal = number(square, 0) == number(square, 1)
    bounds = jnp.where(diagonal, limits_ref[...].astype(WIDE), 0.0)
    kept = (listed > 0.0) & (rank < jnp.sum(bounds, axis=1, keepdims=True))
    rank = jnp.where(kept, rank, -1.0)
    rank_out[...] = rank
    weight_out[...] = weight
    spread = mul(owner, rank.astype(LOW))
    tokens = tokens_ref[...]
    lanes = tokens.shape[1] // 2
    picked = jnp.concatenate([low_if(spread == left), low_if(spread == right)], axis=1)
    sides = jnp.concatenate([tokens[:, :lanes], tokens[:, lanes:]], axis=0)
    tok_out[...] = mul(picked, sides).reshape(experts, chunk, lanes).astype(LOW)


def grad_kernel(pad, rank_ref, weight_ref, clip_ref, cot_ref, cot_out):
    experts, tok_rows = rank_ref.shape
    chunk = 2 * pad
    slots = experts * chunk
    owner = owners((slots, experts), 0, chunk)
    left, right = wanted((slots, tok_rows), 0, pad)
    spread = mul(owner, rank_ref[...].astype(LOW))
    high, rest = split_low(weight_ref[...] * clip_ref[...].astype(WIDE))
    high, rest = mul(owner, high), mul(owner, rest)
    coefs = jnp.concatenate(
        [
            jnp.where(spread == place, part, 0.0).astype(LOW)
            for part in (high, rest)
            for place in (left, right)
        ],
        axis=1,
    )
    cot = cot_ref[...]
    lanes = cot.shape[1] // 2
    sides = jnp.concatenate([cot[:, :lanes], cot[:, lanes:]] * 2, axis=0)
    cot_out[...] = mul(coefs, sides).reshape(experts, chunk, lanes).astype(LOW)


def table_kernel(capacity, rank_ref, weight_ref, pick_out, weight_out):
    experts, tok_rows = rank_ref.shape
    slots = experts * capacity
    owner = owners((experts, slots), 1, capacity)
    place = remainder(number((1, slots), 1), capacity)
    picked = mul(rank_ref[...].T.astype(LOW), owner) == place
    pick_out[...] = low_if(picked)
    for at, part in enumerate(split_low(weight_ref[...].T)):
        weight_out[at * tok_rows : (at + 1) * tok_rows, :] = jnp.where(
            picked, mul(part, owner), 0.0
        ).astype(LOW)


def places(group, capacity, transposed):
    size = 4 * group * capacity
    chunked = number((1, size) if transposed else (size, 1), 1 if transposed else 0)
    expert = jnp.floor((chunked + 0.5) * (1.0 / (4 * capacity)))
    within = chunked - 4 * capacity * expert
    piece = jnp.floor((within + 0.5) * (1.0 / capacity))
    stacked = within - capacity * piece + capacity * (expert + group * piece)
    return low_if(number((size, size), 0 if transposed else 1) == stacked)


def shifts(shape, row_axis, capacity, pad, side):
    row = number(shape, row_axis)
    block = jnp.floor((row + 0.5) * (1.0 / capacity))
    return low_if(
        number(shape, 1 - row_axis) == row + (2 * pad - capacity) * block + pad * side
    )


GROUP = 8


def unpack_kernel(capacity, pad, core_ref, chunks_ref, keep_out, give_out):
    lanes = chunks_ref.shape[2]
    half = chunks_ref.shape[0] // 2
    rows, slots = GROUP * capacity, GROUP * 2 * pad
    moves = [shifts((rows, slots), 0, capacity, pad, side) for side in range(2)]
    core = core_ref[0]
    for out_ref, base in ((keep_out, core * half), (give_out, (1 - core) * half)):
        for at in range(half // GROUP):
            chunk = chunks_ref[pl.ds(base + at * GROUP, GROUP)].reshape(slots, lanes)
            for side in range(2):
                out_ref[at * rows : (at + 1) * rows, side * lanes : (side + 1) * lanes] = mul(
                    moves[side], chunk
                ).astype(LOW)


def pack_kernel(
    capacity,
    core_ref,
    parity_ref,
    out_mine_ref,
    out_got_ref,
    same_mine_ref,
    same_got_ref,
    near_mine_ref,
    near_got_ref,
    chunks_out,
):
    lanes = chunks_out.shape[2]
    half = chunks_out.shape[0] // 2
    rows = GROUP * capacity
    moves = places(GROUP, capacity, False)
    core = core_ref[0]
    odd = parity_ref[0] == 1
    for out_ref, same_ref, near_ref, base in (
        (out_mine_ref, same_mine_ref, near_mine_ref, core * half),
        (out_got_ref, same_got_ref, near_got_ref, (1 - core) * half),
    ):
        for at in range(half // GROUP):
            same, near = same_ref[at].astype(WIDE), near_ref[at].astype(WIDE)
            grads = jnp.concatenate(
                [jnp.where(odd, near, same), jnp.where(odd, same, near)], axis=0
            ).astype(LOW)
            outs = out_ref[at * rows : (at + 1) * rows, :]
            stacked = jnp.concatenate(
                [outs[:, :lanes], outs[:, lanes:], grads[:, :lanes], grads[:, lanes:]], axis=0
            )
            chunks_out[pl.ds(base + at * GROUP, GROUP)] = (
                mul(moves, stacked).reshape(GROUP, 4 * capacity, lanes).astype(LOW)
            )


def merge_kernel(
    capacity, chunks_ref, pick_ref, weight_ref, layer_out, token_out, out_rows, grad_rows
):
    experts, _, lanes = chunks_ref.shape
    tok_rows = layer_out.shape[0]
    rows = GROUP * capacity
    moves = places(GROUP, capacity, True)
    for at in range(experts // GROUP):
        chunk = chunks_ref[at * GROUP : (at + 1) * GROUP].reshape(4 * rows, lanes)
        pieces = mul(moves, chunk).astype(LOW)
        for piece in range(4):
            target = (out_rows, grad_rows)[piece // 2]
            cols = slice(piece % 2 * lanes, (piece % 2 + 1) * lanes)
            target[at * rows : (at + 1) * rows, cols] = pieces[piece * rows : (piece + 1) * rows]
    sums = mul(weight_ref[...], out_rows[...])
    layer_out[...] = (sums[:tok_rows] + sums[tok_rows:]).astype(LOW)
    token_out[...] = mul(pick_ref[...], grad_rows[...]).astype(LOW)


def gate_up_kernel(keep_ref, got_ref, gate_ref, up_ref, other_ref, out_ref):
    ff = gate_ref.shape[1]
    keep, got = keep_ref[...], got_ref[...]
    for at, own_ref in enumerate((gate_ref, up_ref)):
        cols = slice(at * ff, (at + 1) * ff)
        out_ref[:, cols] = (mul(keep, own_ref[...]) + mul(got, other_ref[:, cols])).astype(LOW)


def hidden_grad_kernel(parity_ref, keep_ref, got_ref, own_ref, other_ref, stay_out, leave_out):
    block = stay_out.shape[1]
    parts = against(keep_ref[...], own_ref[...]) + against(got_ref[...], other_ref[...])
    odd = parity_ref[0] == 1
    for at in range(stay_out.shape[0]):
        first = parts[2 * at * block : (2 * at + 1) * block]
        second = parts[(2 * at + 1) * block : (2 * at + 2) * block]
        stay_out[at] = jnp.where(odd, second, first).astype(LOW)
        leave_out[at] = jnp.where(odd, first, second).astype(LOW)


def hidden_kernel(shares_ref, hidden_out):
    ff = shares_ref.shape[1] // 2
    active, _ = swish_parts(shares_ref[:, :ff].astype(WIDE))
    hidden_out[:, :ff] = (active * shares_ref[:, ff:].astype(WIDE)).astype(LOW)
    hidden_out[:, ff:] = jnp.zeros((shares_ref.shape[0], hidden_out.shape[1] - ff), LOW)


def derived_kernel(shares_ref, parts_ref, derived_out):
    ff = parts_ref.shape[2]
    up_val = shares_ref[:, ff:].astype(WIDE)
    grad_hidden = parts_ref[0].astype(WIDE)
    for at in range(1, parts_ref.shape[0]):
        grad_hidden = grad_hidden + parts_ref[at].astype(WIDE)
    active, slope = swish_parts(shares_ref[:, :ff].astype(WIDE))
    derived_out[:, :ff] = (grad_hidden * up_val * slope).astype(LOW)
    derived_out[:, ff:] = (grad_hidden * active).astype(LOW)


def input_kernel(rows_ref, own_ref, other_ref, mine_out, give_out):
    rows = rows_ref[...]
    give_out[...] = against(rows, other_ref[...]).reshape(give_out.shape).astype(LOW)
    mine_out[...] = against(rows, own_ref[...]).reshape(mine_out.shape).astype(LOW)


def body(
    tokens, routes, combine, clip_mask, limits, cotangent, gate_weight, up_weight, down_weight
):
    tok_rows, top_count = routes.shape
    experts = limits.shape[0]
    capacity = 9 * tok_rows * top_count // (8 * experts)
    pad = -(-capacity // 4) * 4
    half = experts * capacity // 2
    width = tokens.shape[1]
    lanes = width // 2
    slots = experts * capacity
    ff = gate_weight.shape[2]
    devices = lax.axis_size("dp")
    chips = devices // 2
    spot = lax.axis_index("dp").astype(jnp.int32)
    core = (spot % 2).reshape(1)
    parity = (spot // 2 % 2).reshape(1)
    column = [[2 * chip + which for chip in range(chips)] for which in range(2)]
    swap_pairs = [(device, device ^ 1) for device in range(devices)]
    near_pairs = []
    for chip in range(chips):
        near_pairs.append((2 * chip, 2 * (chip ^ 1)))
        near_pairs.append((2 * chip + 1, 2 * ((((chip - 1) ^ 1) + 1) % chips) + 1))
    alike = [
        [2 * chip + which for chip in range(first, chips, 2)] for which in range(2) for first in range(2)
    ]
    chunk_shape = jax.ShapeDtypeStruct((experts, 2 * pad, lanes), LOW)
    rank_shape = jax.ShapeDtypeStruct((experts, tok_rows), WIDE)
    half_shape = jax.ShapeDtypeStruct((half, width), LOW)
    tok_shape = jax.ShapeDtypeStruct((tok_rows, width), LOW)
    in_smem = pl.BlockSpec(memory_space=pltpu.SMEM)
    in_vmem = pl.BlockSpec(memory_space=pltpu.VMEM)
    anywhere = pl.BlockSpec(memory_space=pl.ANY)
    params = pltpu.CompilerParams(vmem_limit_bytes=40 * 1024 * 1024)

    def swap(values):
        return lax.ppermute(values, "dp", swap_pairs)

    def exchange(chunks):
        return lax.all_to_all(chunks, "expert", split_axis=0, concat_axis=0, tiled=True)

    def unpack(chunks):
        keep, give = pl.pallas_call(
            functools.partial(unpack_kernel, capacity, pad),
            out_shape=(half_shape, half_shape),
            in_specs=[in_smem, in_vmem],
            compiler_params=params,
            name="unpack",
        )(core, chunks)
        return keep, swap(give)

    gate_own, up_own, down_own = gate_weight[0], up_weight[0], down_weight[0]
    gu_own = jnp.concatenate([gate_own, up_own], axis=1)
    gu_other = swap(gu_own)
    down_other = swap(down_own)

    token_send, rank, weight = pl.pallas_call(
        functools.partial(token_kernel, pad),
        out_shape=(chunk_shape, rank_shape, rank_shape),
        in_specs=[anywhere] * 4,
        scratch_shapes=[
            pltpu.VMEM((top_count, tok_rows), jnp.int32),
            pltpu.VMEM((top_count, tok_rows), WIDE),
            pltpu.VMEM((1, experts), jnp.int32),
            pltpu.VMEM((tok_rows, width), LOW),
            pltpu.SemaphoreType.DMA((4,)),
        ],
        compiler_params=pltpu.CompilerParams(vmem_limit_bytes=63 * 1024 * 1024),
        name="token_rows",
    )(routes.T, combine.T, limits.reshape(1, experts), tokens)
    grad_send = pl.pallas_call(
        functools.partial(grad_kernel, pad),
        out_shape=chunk_shape,
        compiler_params=params,
        name="grad_rows",
    )(rank, weight, clip_mask.reshape(1, tok_rows), cotangent)
    token_chunks, grad_send = lax.optimization_barrier((exchange(token_send), grad_send))
    token_keep, token_got = unpack(token_chunks)
    gate_up = pl.pallas_call(
        gate_up_kernel,
        out_shape=jax.ShapeDtypeStruct((half, 2 * ff), LOW),
        compiler_params=params,
        name="gate_up",
    )(token_keep, token_got, gate_own, up_own, gu_other)
    gate_up, grad_send = lax.optimization_barrier((gate_up, grad_send))
    shares = lax.psum_scatter(
        gate_up, "dp", scatter_dimension=0, tiled=True, axis_index_groups=column
    )
    grad_keep, grad_got = unpack(exchange(grad_send))
    part_shape = jax.ShapeDtypeStruct((chips // 2, half // chips, ff), LOW)
    stay, leave = pl.pallas_call(
        hidden_grad_kernel,
        out_shape=(part_shape, part_shape),
        in_specs=[in_smem] + [in_vmem] * 4,
        compiler_params=params,
        name="hidden_grad",
    )(parity, grad_keep, grad_got, down_own, down_other)
    joined = (stay.astype(WIDE) + lax.ppermute(leave, "dp", near_pairs).astype(WIDE)).astype(LOW)
    share_rows = half // chips
    hidden = pl.pallas_call(
        hidden_kernel,
        out_shape=jax.ShapeDtypeStruct((share_rows, 4 * ff // 3), LOW),
        compiler_params=params,
        name="hidden",
    )(shares)
    hidden, joined = lax.optimization_barrier((hidden, joined))
    hidden_full = lax.all_gather(
        hidden, "dp", axis=0, tiled=True, axis_index_groups=column
    )[:, :ff]
    grad_parts = lax.all_to_all(
        joined, "dp", split_axis=0, concat_axis=0, tiled=True, axis_index_groups=alike
    )
    derived = pl.pallas_call(
        derived_kernel,
        out_shape=jax.ShapeDtypeStruct((share_rows, 2 * ff), LOW),
        compiler_params=params,
        name="derived",
    )(shares, grad_parts)
    same_rows = lax.all_gather(derived, "dp", axis=0, tiled=True, axis_index_groups=alike)
    near_rows = lax.ppermute(same_rows, "dp", near_pairs)
    block_shape = jax.ShapeDtypeStruct((chips // 2, share_rows, width), LOW)

    def input_rows(rows):
        mine, give = pl.pallas_call(
            input_kernel,
            out_shape=(block_shape, block_shape),
            compiler_params=params,
            name="input_rows",
        )(rows, gu_own, gu_other)
        return mine, swap(give)

    same_mine, same_got = input_rows(same_rows)
    near_mine, near_got = input_rows(near_rows)
    out_got = swap(mul(hidden_full, down_other).astype(LOW))
    out_mine = mul(hidden_full, down_own).astype(LOW)
    back = exchange(
        pl.pallas_call(
            functools.partial(pack_kernel, capacity),
            out_shape=jax.ShapeDtypeStruct((experts, 4 * capacity, lanes), LOW),
            in_specs=[in_smem] * 2 + [in_vmem] * 6,
            compiler_params=params,
            name="pack",
        )(core, parity, out_mine, out_got, same_mine, same_got, near_mine, near_got)
    )

    same_blocks = same_rows.reshape(chips // 2, share_rows, 2 * ff)
    near_blocks = near_rows.reshape(chips // 2, share_rows, 2 * ff)
    derived_full = jnp.where(
        parity[0] == 0,
        jnp.stack([same_blocks, near_blocks], axis=1),
        jnp.stack([near_blocks, same_blocks], axis=1),
    ).reshape(half, 2 * ff)
    lower_got = swap(outer(hidden_full, grad_got).astype(LOW))
    down_grads = (outer(hidden_full, grad_keep) + lower_got.astype(WIDE)).astype(LOW)
    upper_got = swap(outer(token_got, derived_full).astype(LOW)).astype(WIDE)
    gate_grads = (outer(token_keep, derived_full[:, :ff]) + upper_got[:, :ff]).astype(LOW)
    up_grads = (outer(token_keep, derived_full[:, ff:]) + upper_got[:, ff:]).astype(LOW)

    picks, weights = pl.pallas_call(
        functools.partial(table_kernel, capacity),
        out_shape=(
            jax.ShapeDtypeStruct((tok_rows, slots), LOW),
            jax.ShapeDtypeStruct((2 * tok_rows, slots), LOW),
        ),
        compiler_params=params,
        name="tables",
    )(rank, weight)
    rows_scratch = pltpu.VMEM((slots, width), LOW)
    layer_out, token_grads = pl.pallas_call(
        functools.partial(merge_kernel, capacity),
        out_shape=(tok_shape, tok_shape),
        scratch_shapes=[rows_scratch, rows_scratch],
        compiler_params=params,
        name="merge",
    )(back, picks, weights)
    return (layer_out, token_grads, gate_grads[None], up_grads[None], down_grads[None])


def solution(mesh):
    in_specs = (
        P("expert", "dp"),
        P("expert", None),
        P("expert", None),
        P("expert"),
        P(),
        P("expert", "dp"),
        P("expert", "dp", None),
        P("expert", "dp", None),
        P("expert", None, "dp"),
    )
    out_specs = (
        P("expert", "dp"),
        P("expert", "dp"),
        P("expert", "dp", None),
        P("expert", "dp", None),
        P("expert", None, "dp"),
    )
    return jax.shard_map(body, mesh=mesh, in_specs=in_specs, out_specs=out_specs, check_vma=False)
```

```python
import functools

import jax
import jax.numpy as jnp
from jax import lax
from jax.experimental import pallas as pl
from jax.experimental.pallas import tpu as pltpu
from jax.sharding import PartitionSpec as P

LOW = jnp.bfloat16
WIDE = jnp.float32


def swish_parts(gate_val):
    sigma = jax.nn.sigmoid(gate_val)
    return (gate_val * sigma, sigma * (1.0 + gate_val * (1.0 - sigma)))


def mul(left, right):
    return jnp.dot(left, right, preferred_element_type=WIDE)


def split_low(values):
    high = values.astype(LOW)
    return high, (values - high.astype(WIDE)).astype(LOW)


def outer(left, right):
    return lax.dot_general(left, right, (((0,), (0,)), ((), ())), preferred_element_type=WIDE)


def against(left, right):
    return lax.dot_general(left, right, (((1,), (1,)), ((), ())), preferred_element_type=WIDE)


def number(shape, axis):
    return lax.broadcasted_iota(jnp.int32, shape, axis).astype(WIDE)


def low_if(condition):
    return jnp.where(condition, 1.0, 0.0).astype(LOW)


def remainder(values, step):
    return values - step * jnp.floor((values + 0.5) * (1.0 / step))


def owners(shape, slot_axis, chunk):
    offset = number(shape, slot_axis) - chunk * number(shape, 1 - slot_axis)
    return low_if((offset >= 0.0) & (offset < chunk))


def wanted(shape, slot_axis, pad):
    within = remainder(number(shape, slot_axis), 2 * pad)
    left = jnp.where(within < pad, within, -5.0)
    right = jnp.where(within >= pad, within - pad, -5.0)
    return left, right


def token_kernel(
    pad,
    routes_hbm,
    combine_hbm,
    limits_hbm,
    tokens_hbm,
    tok_out,
    rank_out,
    weight_out,
    routes_ref,
    combine_ref,
    limits_ref,
    tokens_ref,
    sems,
):
    copies = [
        pltpu.make_async_copy(source, target, sems.at[at])
        for at, (source, target) in enumerate(
            (
                (routes_hbm, routes_ref),
                (combine_hbm, combine_ref),
                (limits_hbm, limits_ref),
                (tokens_hbm, tokens_ref),
            )
        )
    ]
    for copy in copies:
        copy.start()
    top_count, tok_rows = routes_ref.shape
    experts = limits_ref.shape[1]
    chunk = 2 * pad
    slots = experts * chunk
    owner = owners((slots, experts), 0, chunk)
    left, right = wanted((slots, tok_rows), 0, pad)
    before = number((tok_rows, tok_rows), 0) < number((tok_rows, tok_rows), 1)
    square = (experts, experts)
    for copy in copies:
        copy.wait()
    labels = lax.broadcasted_iota(jnp.int32, (experts, tok_rows), 0)
    listed = jnp.zeros((experts, tok_rows), WIDE)
    weight = jnp.zeros((experts, tok_rows), WIDE)
    for entry in range(top_count):
        match = routes_ref[entry : entry + 1, :] == labels
        listed = jnp.where(match, 1.0, listed)
        weight = jnp.where(match, combine_ref[entry : entry + 1, :], weight)
    rank = mul(listed.astype(LOW), low_if(before))
    diagonal = number(square, 0) == number(square, 1)
    bounds = jnp.where(diagonal, limits_ref[...].astype(WIDE), 0.0)
    kept = (listed > 0.0) & (rank < jnp.sum(bounds, axis=1, keepdims=True))
    rank = jnp.where(kept, rank, -1.0)
    rank_out[...] = rank
    weight_out[...] = weight
    spread = mul(owner, rank.astype(LOW))
    tokens = tokens_ref[...]
    lanes = tokens.shape[1] // 2
    picked = jnp.concatenate([low_if(spread == left), low_if(spread == right)], axis=1)
    sides = jnp.concatenate([tokens[:, :lanes], tokens[:, lanes:]], axis=0)
    tok_out[...] = mul(picked, sides).reshape(experts, chunk, lanes).astype(LOW)


def grad_kernel(pad, rank_ref, weight_ref, clip_ref, cot_ref, cot_out):
    experts, tok_rows = rank_ref.shape
    chunk = 2 * pad
    slots = experts * chunk
    owner = owners((slots, experts), 0, chunk)
    left, right = wanted((slots, tok_rows), 0, pad)
    spread = mul(owner, rank_ref[...].astype(LOW))
    high, rest = split_low(weight_ref[...] * clip_ref[...].astype(WIDE))
    high, rest = mul(owner, high), mul(owner, rest)
    coefs = jnp.concatenate(
        [
            jnp.where(spread == place, part, 0.0).astype(LOW)
            for part in (high, rest)
            for place in (left, right)
        ],
        axis=1,
    )
    cot = cot_ref[...]
    lanes = cot.shape[1] // 2
    sides = jnp.concatenate([cot[:, :lanes], cot[:, lanes:]] * 2, axis=0)
    cot_out[...] = mul(coefs, sides).reshape(experts, chunk, lanes).astype(LOW)


def table_kernel(capacity, rank_ref, weight_ref, pick_out, weight_out):
    experts, tok_rows = rank_ref.shape
    slots = experts * capacity
    owner = owners((experts, slots), 1, capacity)
    place = remainder(number((1, slots), 1), capacity)
    picked = mul(rank_ref[...].T.astype(LOW), owner) == place
    pick_out[...] = low_if(picked)
    for at, part in enumerate(split_low(weight_ref[...].T)):
        weight_out[at * tok_rows : (at + 1) * tok_rows, :] = jnp.where(
            picked, mul(part, owner), 0.0
        ).astype(LOW)


def places(group, capacity, transposed):
    size = 4 * group * capacity
    chunked = number((1, size) if transposed else (size, 1), 1 if transposed else 0)
    expert = jnp.floor((chunked + 0.5) * (1.0 / (4 * capacity)))
    within = chunked - 4 * capacity * expert
    piece = jnp.floor((within + 0.5) * (1.0 / capacity))
    stacked = within - capacity * piece + capacity * (expert + group * piece)
    return low_if(number((size, size), 0 if transposed else 1) == stacked)


def shifts(shape, row_axis, capacity, pad, side):
    row = number(shape, row_axis)
    block = jnp.floor((row + 0.5) * (1.0 / capacity))
    return low_if(
        number(shape, 1 - row_axis) == row + (2 * pad - capacity) * block + pad * side
    )


GROUP = 8


def unpack_kernel(capacity, pad, core_ref, chunks_ref, keep_out, give_out):
    lanes = chunks_ref.shape[2]
    half = chunks_ref.shape[0] // 2
    rows, slots = GROUP * capacity, GROUP * 2 * pad
    moves = [shifts((rows, slots), 0, capacity, pad, side) for side in range(2)]
    core = core_ref[0]
    for out_ref, base in ((keep_out, core * half), (give_out, (1 - core) * half)):
        for at in range(half // GROUP):
            chunk = chunks_ref[pl.ds(base + at * GROUP, GROUP)].reshape(slots, lanes)
            for side in range(2):
                out_ref[at * rows : (at + 1) * rows, side * lanes : (side + 1) * lanes] = mul(
                    moves[side], chunk
                ).astype(LOW)


def pack_kernel(capacity, core_ref, mine_ref, got_ref, chunks_out):
    lanes = chunks_out.shape[2]
    half = chunks_out.shape[0] // 2
    rows = GROUP * capacity
    moves = places(GROUP, capacity, False)
    core = core_ref[0]
    for in_ref, base in ((mine_ref, core * half), (got_ref, (1 - core) * half)):
        for at in range(half // GROUP):
            stacked = jnp.concatenate(
                [
                    in_ref[first + at * rows : first + (at + 1) * rows, cols]
                    for first in (0, half * capacity)
                    for cols in (slice(0, lanes), slice(lanes, 2 * lanes))
                ],
                axis=0,
            )
            chunks_out[pl.ds(base + at * GROUP, GROUP)] = (
                mul(moves, stacked).reshape(GROUP, 4 * capacity, lanes).astype(LOW)
            )


def merge_kernel(
    capacity, chunks_ref, pick_ref, weight_ref, layer_out, token_out, out_rows, grad_rows
):
    experts, _, lanes = chunks_ref.shape
    tok_rows = layer_out.shape[0]
    rows = GROUP * capacity
    moves = places(GROUP, capacity, True)
    for at in range(experts // GROUP):
        chunk = chunks_ref[at * GROUP : (at + 1) * GROUP].reshape(4 * rows, lanes)
        pieces = mul(moves, chunk).astype(LOW)
        for piece in range(4):
            target = (out_rows, grad_rows)[piece // 2]
            cols = slice(piece % 2 * lanes, (piece % 2 + 1) * lanes)
            target[at * rows : (at + 1) * rows, cols] = pieces[piece * rows : (piece + 1) * rows]
    sums = mul(weight_ref[...], out_rows[...])
    layer_out[...] = (sums[:tok_rows] + sums[tok_rows:]).astype(LOW)
    token_out[...] = mul(pick_ref[...], grad_rows[...]).astype(LOW)


def gate_up_kernel(keep_ref, got_ref, gate_ref, up_ref, other_ref, out_ref):
    ff = gate_ref.shape[1]
    keep, got = keep_ref[...], got_ref[...]
    for at, own_ref in enumerate((gate_ref, up_ref)):
        cols = slice(at * ff, (at + 1) * ff)
        out_ref[:, cols] = (mul(keep, own_ref[...]) + mul(got, other_ref[:, cols])).astype(LOW)


def hidden_grad_kernel(parity_ref, keep_ref, got_ref, own_ref, other_ref, stay_out, leave_out):
    block = stay_out.shape[1]
    parts = against(keep_ref[...], own_ref[...]) + against(got_ref[...], other_ref[...])
    odd = parity_ref[0] == 1
    for at in range(stay_out.shape[0]):
        first = parts[2 * at * block : (2 * at + 1) * block]
        second = parts[(2 * at + 1) * block : (2 * at + 2) * block]
        stay_out[at] = jnp.where(odd, second, first).astype(LOW)
        leave_out[at] = jnp.where(odd, first, second).astype(LOW)


def total_kernel(parts_ref, out_ref):
    total = parts_ref[0].astype(WIDE)
    for at in range(1, parts_ref.shape[0]):
        total = total + parts_ref[at].astype(WIDE)
    out_ref[...] = total.astype(LOW)


def give_kernel(
    shares_ref, grad_ref, gu_ref, down_ref, hidden_out, derived_out, give_out
):
    half, ff = grad_ref.shape
    step = GROUP * (half // 4 // GROUP)
    for start in range(0, half, step):
        rows = slice(start, start + step)
        gate_val = shares_ref[rows, :ff].astype(WIDE)
        up_val = shares_ref[rows, ff:].astype(WIDE)
        grad_hidden = grad_ref[rows, :].astype(WIDE)
        active, slope = swish_parts(gate_val)
        hidden_out[rows, :] = (active * up_val).astype(LOW)
        derived_out[rows, :ff] = (grad_hidden * up_val * slope).astype(LOW)
        derived_out[rows, ff:] = (grad_hidden * active).astype(LOW)
    give_out[:half, :] = mul(hidden_out[...], down_ref[...]).astype(LOW)
    give_out[half:, :] = against(derived_out[...], gu_ref[...]).astype(LOW)


def mine_kernel(hidden_ref, derived_ref, gu_ref, down_ref, mine_out):
    half = hidden_ref.shape[0]
    mine_out[:half, :] = mul(hidden_ref[...], down_ref[...]).astype(LOW)
    mine_out[half:, :] = against(derived_ref[...], gu_ref[...]).astype(LOW)


def body(
    tokens, routes, combine, clip_mask, limits, cotangent, gate_weight, up_weight, down_weight
):
    tok_rows, top_count = routes.shape
    experts = limits.shape[0]
    capacity = 9 * tok_rows * top_count // (8 * experts)
    pad = -(-capacity // 4) * 4
    half = experts * capacity // 2
    width = tokens.shape[1]
    lanes = width // 2
    slots = experts * capacity
    ff = gate_weight.shape[2]
    devices = lax.axis_size("dp")
    chips = devices // 2
    spot = lax.axis_index("dp").astype(jnp.int32)
    core = (spot % 2).reshape(1)
    parity = (spot // 2 % 2).reshape(1)
    column = [[2 * chip + which for chip in range(chips)] for which in range(2)]
    swap_pairs = [(device, device ^ 1) for device in range(devices)]
    near_pairs = []
    for chip in range(chips):
        near_pairs.append((2 * chip, 2 * (chip ^ 1)))
        near_pairs.append((2 * chip + 1, 2 * ((((chip - 1) ^ 1) + 1) % chips) + 1))
    alike = [
        [2 * chip + which for chip in range(first, chips, 2)] for which in range(2) for first in range(2)
    ]
    chunk_shape = jax.ShapeDtypeStruct((experts, 2 * pad, lanes), LOW)
    rank_shape = jax.ShapeDtypeStruct((experts, tok_rows), WIDE)
    half_shape = jax.ShapeDtypeStruct((half, width), LOW)
    tok_shape = jax.ShapeDtypeStruct((tok_rows, width), LOW)
    in_smem = pl.BlockSpec(memory_space=pltpu.SMEM)
    in_vmem = pl.BlockSpec(memory_space=pltpu.VMEM)
    anywhere = pl.BlockSpec(memory_space=pl.ANY)
    params = pltpu.CompilerParams(vmem_limit_bytes=40 * 1024 * 1024)

    def swap(values):
        return lax.ppermute(values, "dp", swap_pairs)

    def exchange(chunks):
        return lax.all_to_all(chunks, "expert", split_axis=0, concat_axis=0, tiled=True)

    def unpack(chunks):
        keep, give = pl.pallas_call(
            functools.partial(unpack_kernel, capacity, pad),
            out_shape=(half_shape, half_shape),
            in_specs=[in_smem, in_vmem],
            compiler_params=params,
            name="unpack",
        )(core, chunks)
        return keep, swap(give)

    gate_own, up_own, down_own = gate_weight[0], up_weight[0], down_weight[0]
    gu_own = jnp.concatenate([gate_own, up_own], axis=1)
    gu_other = swap(gu_own)
    down_other = swap(down_own)

    token_send, rank, weight = pl.pallas_call(
        functools.partial(token_kernel, pad),
        out_shape=(chunk_shape, rank_shape, rank_shape),
        in_specs=[anywhere] * 4,
        scratch_shapes=[
            pltpu.VMEM((top_count, tok_rows), jnp.int32),
            pltpu.VMEM((top_count, tok_rows), WIDE),
            pltpu.VMEM((1, experts), jnp.int32),
            pltpu.VMEM((tok_rows, width), LOW),
            pltpu.SemaphoreType.DMA((4,)),
        ],
        compiler_params=pltpu.CompilerParams(vmem_limit_bytes=63 * 1024 * 1024),
        name="token_rows",
    )(routes.T, combine.T, limits.reshape(1, experts), tokens)
    grad_send = pl.pallas_call(
        functools.partial(grad_kernel, pad),
        out_shape=chunk_shape,
        compiler_params=params,
        name="grad_rows",
    )(rank, weight, clip_mask.reshape(1, tok_rows), cotangent)
    token_chunks, grad_send = lax.optimization_barrier((exchange(token_send), grad_send))
    token_keep, token_got = unpack(token_chunks)
    gate_up = pl.pallas_call(
        gate_up_kernel,
        out_shape=jax.ShapeDtypeStruct((half, 2 * ff), LOW),
        compiler_params=params,
        name="gate_up",
    )(token_keep, token_got, gate_own, up_own, gu_other)
    gate_up, grad_send = lax.optimization_barrier((gate_up, grad_send))
    shares = lax.psum_scatter(
        gate_up, "dp", scatter_dimension=0, tiled=True, axis_index_groups=column
    )
    grad_keep, grad_got = unpack(exchange(grad_send))
    part_shape = jax.ShapeDtypeStruct((chips // 2, half // chips, ff), LOW)
    stay, leave = pl.pallas_call(
        hidden_grad_kernel,
        out_shape=(part_shape, part_shape),
        in_specs=[in_smem] + [in_vmem] * 4,
        compiler_params=params,
        name="hidden_grad",
    )(parity, grad_keep, grad_got, down_own, down_other)
    joined = (stay.astype(WIDE) + lax.ppermute(leave, "dp", near_pairs).astype(WIDE)).astype(LOW)
    shares, joined = lax.optimization_barrier((shares, joined))
    shares_full = lax.all_gather(shares, "dp", axis=0, tiled=True, axis_index_groups=column)
    grad_parts = lax.all_to_all(
        joined, "dp", split_axis=0, concat_axis=0, tiled=True, axis_index_groups=alike
    )
    grad_total = pl.pallas_call(
        total_kernel,
        out_shape=jax.ShapeDtypeStruct((half // chips, ff), LOW),
        compiler_params=params,
        name="total",
    )(grad_parts)
    grad_full = lax.all_gather(grad_total, "dp", axis=0, tiled=True, axis_index_groups=column)
    pair_shape = jax.ShapeDtypeStruct((2 * half, width), LOW)
    hidden_full, derived_full, give = pl.pallas_call(
        give_kernel,
        out_shape=(
            jax.ShapeDtypeStruct((half, ff), LOW),
            jax.ShapeDtypeStruct((half, 2 * ff), LOW),
            pair_shape,
        ),
        compiler_params=params,
        name="give_rows",
    )(shares_full, grad_full, gu_other, down_other)
    mine = pl.pallas_call(
        mine_kernel,
        out_shape=pair_shape,
        compiler_params=params,
        name="mine_rows",
    )(hidden_full, derived_full, gu_own, down_own)
    back = exchange(
        pl.pallas_call(
            functools.partial(pack_kernel, capacity),
            out_shape=jax.ShapeDtypeStruct((experts, 4 * capacity, lanes), LOW),
            in_specs=[in_smem] + [in_vmem] * 2,
            compiler_params=params,
            name="pack",
        )(core, mine, swap(give))
    )

    lower_got = swap(outer(hidden_full, grad_got).astype(LOW))
    down_grads = (outer(hidden_full, grad_keep) + lower_got.astype(WIDE)).astype(LOW)
    upper_got = swap(outer(token_got, derived_full).astype(LOW)).astype(WIDE)
    gate_grads = (outer(token_keep, derived_full[:, :ff]) + upper_got[:, :ff]).astype(LOW)
    up_grads = (outer(token_keep, derived_full[:, ff:]) + upper_got[:, ff:]).astype(LOW)

    picks, weights = pl.pallas_call(
        functools.partial(table_kernel, capacity),
        out_shape=(
            jax.ShapeDtypeStruct((tok_rows, slots), LOW),
            jax.ShapeDtypeStruct((2 * tok_rows, slots), LOW),
        ),
        compiler_params=params,
        name="tables",
    )(rank, weight)
    rows_scratch = pltpu.VMEM((slots, width), LOW)
    layer_out, token_grads = pl.pallas_call(
        functools.partial(merge_kernel, capacity),
        out_shape=(tok_shape, tok_shape),
        scratch_shapes=[rows_scratch, rows_scratch],
        compiler_params=params,
        name="merge",
    )(back, picks, weights)
    return (layer_out, token_grads, gate_grads[None], up_grads[None], down_grads[None])


def solution(mesh):
    in_specs = (
        P("expert", "dp"),
        P("expert", None),
        P("expert", None),
        P("expert"),
        P(),
        P("expert", "dp"),
        P("expert", "dp", None),
        P("expert", "dp", None),
        P("expert", None, "dp"),
    )
    out_specs = (
        P("expert", "dp"),
        P("expert", "dp"),
        P("expert", "dp", None),
        P("expert", "dp", None),
        P("expert", None, "dp"),
    )
    return jax.shard_map(body, mesh=mesh, in_specs=in_specs, out_specs=out_specs, check_vma=False)
```

```python
import functools

import jax
import jax.numpy as jnp
from jax import lax
from jax.experimental import pallas as pl
from jax.experimental.pallas import tpu as pltpu
from jax.sharding import PartitionSpec as P

LOW = jnp.bfloat16
WIDE = jnp.float32


def swish_parts(gate_val):
    sigma = jax.nn.sigmoid(gate_val)
    return (gate_val * sigma, sigma * (1.0 + gate_val * (1.0 - sigma)))


def mul(left, right):
    return jnp.dot(left, right, preferred_element_type=WIDE)


def split_low(values):
    high = values.astype(LOW)
    return high, (values - high.astype(WIDE)).astype(LOW)


def outer(left, right):
    return lax.dot_general(left, right, (((0,), (0,)), ((), ())), preferred_element_type=WIDE)


def against(left, right):
    return lax.dot_general(left, right, (((1,), (1,)), ((), ())), preferred_element_type=WIDE)


def number(shape, axis):
    return lax.broadcasted_iota(jnp.int32, shape, axis).astype(WIDE)


def low_if(condition):
    return jnp.where(condition, 1.0, 0.0).astype(LOW)


def remainder(values, step):
    return values - step * jnp.floor((values + 0.5) * (1.0 / step))


def owners(shape, slot_axis, chunk):
    offset = number(shape, slot_axis) - chunk * number(shape, 1 - slot_axis)
    return low_if((offset >= 0.0) & (offset < chunk))


def wanted(shape, slot_axis, pad):
    within = remainder(number(shape, slot_axis), 2 * pad)
    left = jnp.where(within < pad, within, -5.0)
    right = jnp.where(within >= pad, within - pad, -5.0)
    return left, right


def token_kernel(
    pad,
    routes_hbm,
    combine_hbm,
    limits_hbm,
    tokens_hbm,
    tok_out,
    rank_out,
    weight_out,
    routes_ref,
    combine_ref,
    limits_ref,
    tokens_ref,
    sems,
):
    copies = [
        pltpu.make_async_copy(source, target, sems.at[at])
        for at, (source, target) in enumerate(
            (
                (routes_hbm, routes_ref),
                (combine_hbm, combine_ref),
                (limits_hbm, limits_ref),
                (tokens_hbm, tokens_ref),
            )
        )
    ]
    for copy in copies:
        copy.start()
    top_count, tok_rows = routes_ref.shape
    experts = limits_ref.shape[1]
    chunk = 2 * pad
    slots = experts * chunk
    owner = owners((slots, experts), 0, chunk)
    left, right = wanted((slots, tok_rows), 0, pad)
    before = number((tok_rows, tok_rows), 0) < number((tok_rows, tok_rows), 1)
    square = (experts, experts)
    for copy in copies:
        copy.wait()
    labels = lax.broadcasted_iota(jnp.int32, (experts, tok_rows), 0)
    listed = jnp.zeros((experts, tok_rows), WIDE)
    weight = jnp.zeros((experts, tok_rows), WIDE)
    for entry in range(top_count):
        match = routes_ref[entry : entry + 1, :] == labels
        listed = jnp.where(match, 1.0, listed)
        weight = jnp.where(match, combine_ref[entry : entry + 1, :], weight)
    rank = mul(listed.astype(LOW), low_if(before))
    diagonal = number(square, 0) == number(square, 1)
    bounds = jnp.where(diagonal, limits_ref[...].astype(WIDE), 0.0)
    kept = (listed > 0.0) & (rank < jnp.sum(bounds, axis=1, keepdims=True))
    rank = jnp.where(kept, rank, -1.0)
    rank_out[...] = rank
    weight_out[...] = weight
    spread = mul(owner, rank.astype(LOW))
    tokens = tokens_ref[...]
    lanes = tokens.shape[1] // 2
    picked = jnp.concatenate([low_if(spread == left), low_if(spread == right)], axis=1)
    sides = jnp.concatenate([tokens[:, :lanes], tokens[:, lanes:]], axis=0)
    tok_out[...] = mul(picked, sides).reshape(experts, chunk, lanes).astype(LOW)


def grad_kernel(pad, rank_ref, weight_ref, clip_ref, cot_ref, cot_out):
    experts, tok_rows = rank_ref.shape
    chunk = 2 * pad
    slots = experts * chunk
    owner = owners((slots, experts), 0, chunk)
    left, right = wanted((slots, tok_rows), 0, pad)
    spread = mul(owner, rank_ref[...].astype(LOW))
    high, rest = split_low(weight_ref[...] * clip_ref[...].astype(WIDE))
    high, rest = mul(owner, high), mul(owner, rest)
    coefs = jnp.concatenate(
        [
            jnp.where(spread == place, part, 0.0).astype(LOW)
            for part in (high, rest)
            for place in (left, right)
        ],
        axis=1,
    )
    cot = cot_ref[...]
    lanes = cot.shape[1] // 2
    sides = jnp.concatenate([cot[:, :lanes], cot[:, lanes:]] * 2, axis=0)
    cot_out[...] = mul(coefs, sides).reshape(experts, chunk, lanes).astype(LOW)


def table_kernel(capacity, rank_ref, weight_ref, table_out):
    experts, tok_rows = rank_ref.shape
    slots = experts * capacity
    owner = owners((experts, slots), 1, capacity)
    place = remainder(number((1, slots), 1), capacity)
    picked = mul(rank_ref[...].T.astype(LOW), owner) == place
    table_out[0:tok_rows, :] = low_if(picked)
    for at, part in enumerate(split_low(weight_ref[...].T)):
        table_out[(at + 1) * tok_rows : (at + 2) * tok_rows, :] = jnp.where(
            picked, mul(part, owner), 0.0
        ).astype(LOW)


def places(group, capacity, transposed):
    size = 4 * group * capacity
    chunked = number((1, size) if transposed else (size, 1), 1 if transposed else 0)
    expert = jnp.floor((chunked + 0.5) * (1.0 / (4 * capacity)))
    within = chunked - 4 * capacity * expert
    piece = jnp.floor((within + 0.5) * (1.0 / capacity))
    stacked = within - capacity * piece + capacity * (expert + group * piece)
    return low_if(number((size, size), 0 if transposed else 1) == stacked)


def shifts(shape, row_axis, capacity, pad, side):
    row = number(shape, row_axis)
    block = jnp.floor((row + 0.5) * (1.0 / capacity))
    return low_if(
        number(shape, 1 - row_axis) == row + (2 * pad - capacity) * block + pad * side
    )


GROUP = 8


def unpack_kernel(capacity, pad, core_ref, chunks_ref, keep_out, give_out):
    lanes = chunks_ref.shape[2]
    half = chunks_ref.shape[0] // 2
    rows, slots = GROUP * capacity, GROUP * 2 * pad
    moves = [shifts((rows, slots), 0, capacity, pad, side) for side in range(2)]
    core = core_ref[0]
    for out_ref, base in ((keep_out, core * half), (give_out, (1 - core) * half)):
        for at in range(half // GROUP):
            chunk = chunks_ref[pl.ds(base + at * GROUP, GROUP)].reshape(slots, lanes)
            for side in range(2):
                out_ref[at * rows : (at + 1) * rows, side * lanes : (side + 1) * lanes] = mul(
                    moves[side], chunk
                ).astype(LOW)


def pack_kernel(capacity, core_ref, mine_ref, got_ref, chunks_out):
    lanes = chunks_out.shape[2]
    half = chunks_out.shape[0] // 2
    rows = GROUP * capacity
    moves = places(GROUP, capacity, False)
    core = core_ref[0]
    for in_ref, base in ((mine_ref, core * half), (got_ref, (1 - core) * half)):
        for at in range(0, half // GROUP, 2):
            stacked = jnp.concatenate(
                [
                    jnp.concatenate(
                        [
                            in_ref[first + now * rows : first + (now + 1) * rows, cols]
                            for now in (at, at + 1)
                        ],
                        axis=1,
                    )
                    for first in (0, half * capacity)
                    for cols in (slice(0, lanes), slice(lanes, 2 * lanes))
                ],
                axis=0,
            )
            moved = mul(moves, stacked)
            for side in range(2):
                chunks_out[pl.ds(base + (at + side) * GROUP, GROUP)] = (
                    moved[:, side * lanes : (side + 1) * lanes]
                    .reshape(GROUP, 4 * capacity, lanes)
                    .astype(LOW)
                )


def merge_kernel(
    capacity,
    chunks_ref,
    table_ref,
    layer_out,
    token_out,
    out_rows,
    grad_rows,
):
    experts, _, lanes = chunks_ref.shape
    tok_rows = layer_out.shape[0]
    rows = GROUP * capacity
    moves = places(GROUP, capacity, True)
    for at in range(0, experts // GROUP, 2):
        chunks = [
            chunks_ref[now * GROUP : (now + 1) * GROUP].reshape(4 * rows, lanes)
            for now in (at, at + 1)
        ]
        pieces = mul(moves, jnp.concatenate(chunks, axis=1)).astype(LOW)
        for piece in range(4):
            target = (out_rows, grad_rows)[piece // 2]
            cols = slice(piece % 2 * lanes, (piece % 2 + 1) * lanes)
            for side in range(2):
                first = (at + side) * rows
                target[first : first + rows, cols] = pieces[
                    piece * rows : (piece + 1) * rows, side * lanes : (side + 1) * lanes
                ]
    sums = mul(table_ref[tok_rows:, :], out_rows[...])
    layer_out[...] = (sums[:tok_rows] + sums[tok_rows:]).astype(LOW)
    token_out[...] = mul(table_ref[0:tok_rows, :], grad_rows[...]).astype(LOW)


def gate_up_kernel(
    keep_ref,
    got_ref,
    gate_ref,
    up_ref,
    other_ref,
    out_hbm,
    out_ref,
    sems,
):
    ff = gate_ref.shape[1]
    step = ff // 3
    copies = []
    keep, got = keep_ref[...], got_ref[...]
    for at in range(6):
        own_ref = (gate_ref, up_ref)[at // 3]
        cols = slice(at * step, (at + 1) * step)
        own_cols = slice(at % 3 * step, (at % 3 + 1) * step)
        out_ref[:, cols] = (mul(keep, own_ref[:, own_cols]) + mul(got, other_ref[:, cols])).astype(
            LOW
        )
        copy = pltpu.make_async_copy(out_ref.at[:, cols], out_hbm.at[:, cols], sems.at[at])
        copy.start()
        copies.append(copy)
    for copy in copies:
        copy.wait()


def hidden_grad_kernel(parity_ref, keep_ref, got_ref, own_ref, other_ref, stay_out, leave_out):
    block = stay_out.shape[1]
    parts = against(keep_ref[...], own_ref[...]) + against(got_ref[...], other_ref[...])
    odd = parity_ref[0] == 1
    for at in range(stay_out.shape[0]):
        first = parts[2 * at * block : (2 * at + 1) * block]
        second = parts[(2 * at + 1) * block : (2 * at + 2) * block]
        stay_out[at] = jnp.where(odd, second, first).astype(LOW)
        leave_out[at] = jnp.where(odd, first, second).astype(LOW)


def total_kernel(parts_ref, out_ref):
    total = parts_ref[0].astype(WIDE)
    for at in range(1, parts_ref.shape[0]):
        total = total + parts_ref[at].astype(WIDE)
    out_ref[...] = total.astype(LOW)


def rows_kernel(
    shares_hbm,
    grad_hbm,
    gu_hbm,
    down_hbm,
    gu_own_hbm,
    down_own_hbm,
    hidden_out,
    derived_out,
    give_out,
    mine_out,
    shares_ref,
    grad_ref,
    gu_ref,
    down_ref,
    gu_own_ref,
    down_own_ref,
    sems,
):
    half, ff = grad_ref.shape
    step = half // 4
    blocks = [slice(at * step, (at + 1) * step) for at in range(4)]
    loads = [
        (
            pltpu.make_async_copy(grad_hbm.at[rows], grad_ref.at[rows], sems.at[6 + at]),
            pltpu.make_async_copy(shares_hbm.at[rows], shares_ref.at[rows], sems.at[at]),
        )
        for at, rows in enumerate(blocks)
    ]
    weights = [
        pltpu.make_async_copy(down_hbm, down_ref, sems.at[4]),
        pltpu.make_async_copy(gu_hbm, gu_ref, sems.at[5]),
        pltpu.make_async_copy(down_own_hbm, down_own_ref, sems.at[10]),
        pltpu.make_async_copy(gu_own_hbm, gu_own_ref, sems.at[11]),
    ]
    for copy in [copy for load in loads for copy in load] + weights:
        copy.start()
    for rows, load in zip(blocks, loads):
        for copy in load:
            copy.wait()
        gate_val = shares_ref[rows, :ff].astype(WIDE)
        up_val = shares_ref[rows, ff:].astype(WIDE)
        grad_hidden = grad_ref[rows, :].astype(WIDE)
        active, slope = swish_parts(gate_val)
        hidden_out[rows, :] = (active * up_val).astype(LOW)
        derived_out[rows, :ff] = (grad_hidden * up_val * slope).astype(LOW)
        derived_out[rows, ff:] = (grad_hidden * active).astype(LOW)
    for copy in weights:
        copy.wait()
    for out_ref, lower_ref, upper_ref in (
        (give_out, down_ref, gu_ref),
        (mine_out, down_own_ref, gu_own_ref),
    ):
        out_ref[:half, :] = mul(hidden_out[...], lower_ref[...]).astype(LOW)
        out_ref[half:, :] = against(derived_out[...], upper_ref[...]).astype(LOW)


def body(
    tokens, routes, combine, clip_mask, limits, cotangent, gate_weight, up_weight, down_weight
):
    tok_rows, top_count = routes.shape
    experts = limits.shape[0]
    capacity = 9 * tok_rows * top_count // (8 * experts)
    pad = -(-capacity // 4) * 4
    half = experts * capacity // 2
    width = tokens.shape[1]
    lanes = width // 2
    slots = experts * capacity
    ff = gate_weight.shape[2]
    devices = lax.axis_size("dp")
    chips = devices // 2
    spot = lax.axis_index("dp").astype(jnp.int32)
    core = (spot % 2).reshape(1)
    parity = (spot // 2 % 2).reshape(1)
    column = [[2 * chip + which for chip in range(chips)] for which in range(2)]
    swap_pairs = [(device, device ^ 1) for device in range(devices)]
    near_pairs = []
    for chip in range(chips):
        near_pairs.append((2 * chip, 2 * (chip ^ 1)))
        near_pairs.append((2 * chip + 1, 2 * ((((chip - 1) ^ 1) + 1) % chips) + 1))
    alike = [
        [2 * chip + which for chip in range(first, chips, 2)] for which in range(2) for first in range(2)
    ]
    chunk_shape = jax.ShapeDtypeStruct((experts, 2 * pad, lanes), LOW)
    rank_shape = jax.ShapeDtypeStruct((experts, tok_rows), WIDE)
    half_shape = jax.ShapeDtypeStruct((half, width), LOW)
    tok_shape = jax.ShapeDtypeStruct((tok_rows, width), LOW)
    in_smem = pl.BlockSpec(memory_space=pltpu.SMEM)
    in_vmem = pl.BlockSpec(memory_space=pltpu.VMEM)
    in_hbm = pl.BlockSpec(memory_space=pltpu.HBM)
    anywhere = pl.BlockSpec(memory_space=pl.ANY)
    params = pltpu.CompilerParams(vmem_limit_bytes=16 * 1024 * 1024)

    def swap(values):
        return lax.ppermute(values, "dp", swap_pairs)

    def exchange(chunks):
        return lax.all_to_all(chunks, "expert", split_axis=0, concat_axis=0, tiled=True)

    def unpack(chunks):
        keep, give = pl.pallas_call(
            functools.partial(unpack_kernel, capacity, pad),
            out_shape=(half_shape, half_shape),
            in_specs=[in_smem, in_vmem],
            compiler_params=params,
            name="unpack",
        )(core, chunks)
        return keep, swap(give)

    gate_own, up_own, down_own = gate_weight[0], up_weight[0], down_weight[0]
    gu_own = jnp.concatenate([gate_own, up_own], axis=1)
    gu_other = swap(gu_own)
    down_other = swap(down_own)

    token_send, rank, weight = pl.pallas_call(
        functools.partial(token_kernel, pad),
        out_shape=(chunk_shape, rank_shape, rank_shape),
        in_specs=[anywhere] * 4,
        scratch_shapes=[
            pltpu.VMEM((top_count, tok_rows), jnp.int32),
            pltpu.VMEM((top_count, tok_rows), WIDE),
            pltpu.VMEM((1, experts), jnp.int32),
            pltpu.VMEM((tok_rows, width), LOW),
            pltpu.SemaphoreType.DMA((4,)),
        ],
        compiler_params=pltpu.CompilerParams(vmem_limit_bytes=63 * 1024 * 1024),
        name="token_rows",
    )(routes.T, combine.T, limits.reshape(1, experts), tokens)
    grad_send = pl.pallas_call(
        functools.partial(grad_kernel, pad),
        out_shape=chunk_shape,
        compiler_params=params,
        name="grad_rows",
    )(rank, weight, clip_mask.reshape(1, tok_rows), cotangent)
    token_chunks, grad_send = lax.optimization_barrier((exchange(token_send), grad_send))
    token_keep, token_got = unpack(token_chunks)
    gate_up = pl.pallas_call(
        gate_up_kernel,
        out_shape=jax.ShapeDtypeStruct((half, 2 * ff), LOW),
        in_specs=[in_vmem] * 5,
        out_specs=in_hbm,
        scratch_shapes=[pltpu.VMEM((half, 2 * ff), LOW), pltpu.SemaphoreType.DMA((6,))],
        compiler_params=params,
        name="gate_up",
    )(token_keep, token_got, gate_own, up_own, gu_other)
    gate_up, grad_send = lax.optimization_barrier((gate_up, grad_send))
    shares = lax.psum_scatter(
        gate_up, "dp", scatter_dimension=0, tiled=True, axis_index_groups=column
    )
    grad_keep, grad_got = unpack(exchange(grad_send))
    part_shape = jax.ShapeDtypeStruct((chips // 2, half // chips, ff), LOW)
    stay, leave = pl.pallas_call(
        hidden_grad_kernel,
        out_shape=(part_shape, part_shape),
        in_specs=[in_smem] + [in_vmem] * 4,
        compiler_params=params,
        name="hidden_grad",
    )(parity, grad_keep, grad_got, down_own, down_other)
    shares, near = lax.optimization_barrier((shares, lax.ppermute(leave, "dp", near_pairs)))
    joined = (stay.astype(WIDE) + near.astype(WIDE)).astype(LOW)
    shares_full = lax.all_gather(shares, "dp", axis=0, tiled=True, axis_index_groups=column)
    grad_parts = lax.all_to_all(
        joined, "dp", split_axis=0, concat_axis=0, tiled=True, axis_index_groups=alike
    )
    grad_total = pl.pallas_call(
        total_kernel,
        out_shape=jax.ShapeDtypeStruct((half // chips, ff), LOW),
        compiler_params=params,
        name="total",
    )(grad_parts)
    grad_full = lax.all_gather(grad_total, "dp", axis=0, tiled=True, axis_index_groups=column)
    pair_shape = jax.ShapeDtypeStruct((2 * half, width), LOW)
    hidden_full, derived_full, give, mine = pl.pallas_call(
        rows_kernel,
        out_shape=(
            jax.ShapeDtypeStruct((half, ff), LOW),
            jax.ShapeDtypeStruct((half, 2 * ff), LOW),
            pair_shape,
            pair_shape,
        ),
        in_specs=[anywhere] * 6,
        scratch_shapes=[
            pltpu.VMEM((half, 2 * ff), LOW),
            pltpu.VMEM((half, ff), LOW),
            pltpu.VMEM((width, 2 * ff), LOW),
            pltpu.VMEM((ff, width), LOW),
            pltpu.VMEM((width, 2 * ff), LOW),
            pltpu.VMEM((ff, width), LOW),
            pltpu.SemaphoreType.DMA((12,)),
        ],
        compiler_params=pltpu.CompilerParams(vmem_limit_bytes=63 * 1024 * 1024),
        name="expert_rows",
    )(shares_full, grad_full, gu_other, down_other, gu_own, down_own)
    back = exchange(
        pl.pallas_call(
            functools.partial(pack_kernel, capacity),
            out_shape=jax.ShapeDtypeStruct((experts, 4 * capacity, lanes), LOW),
            in_specs=[in_smem] + [in_vmem] * 2,
            compiler_params=params,
            name="pack",
        )(core, mine, swap(give))
    )

    lower_got = swap(outer(hidden_full, grad_got).astype(LOW))
    down_grads = (outer(hidden_full, grad_keep) + lower_got.astype(WIDE)).astype(LOW)
    upper_got = swap(outer(token_got, derived_full).astype(LOW)).astype(WIDE)
    gate_grads = (outer(token_keep, derived_full[:, :ff]) + upper_got[:, :ff]).astype(LOW)
    up_grads = (outer(token_keep, derived_full[:, ff:]) + upper_got[:, ff:]).astype(LOW)

    table = pl.pallas_call(
        functools.partial(table_kernel, capacity),
        out_shape=jax.ShapeDtypeStruct((3 * tok_rows, slots), LOW),
        compiler_params=params,
        name="table",
    )(rank, weight)
    rows_scratch = pltpu.VMEM((slots, width), LOW)
    layer_out, token_grads = pl.pallas_call(
        functools.partial(merge_kernel, capacity),
        out_shape=(tok_shape, tok_shape),
        scratch_shapes=[rows_scratch, rows_scratch],
        compiler_params=params,
        name="merge",
    )(back, table)
    return (layer_out, token_grads, gate_grads[None], up_grads[None], down_grads[None])


def solution(mesh):
    in_specs = (
        P("expert", "dp"),
        P("expert", None),
        P("expert", None),
        P("expert"),
        P(),
        P("expert", "dp"),
        P("expert", "dp", None),
        P("expert", "dp", None),
        P("expert", None, "dp"),
    )
    out_specs = (
        P("expert", "dp"),
        P("expert", "dp"),
        P("expert", "dp", None),
        P("expert", "dp", None),
        P("expert", None, "dp"),
    )
    return jax.shard_map(body, mesh=mesh, in_specs=in_specs, out_specs=out_specs, check_vma=False)
```

```python
import functools

import jax
import jax.numpy as jnp
from jax import lax
from jax.experimental import pallas as pl
from jax.experimental.pallas import tpu as pltpu
from jax.sharding import PartitionSpec as P

LOW = jnp.bfloat16
WIDE = jnp.float32


def swish_parts(gate_val):
    sigma = jax.nn.sigmoid(gate_val)
    return (gate_val * sigma, sigma * (1.0 + gate_val * (1.0 - sigma)))


def mul(left, right):
    return jnp.dot(left, right, preferred_element_type=WIDE)


def split_low(values):
    high = values.astype(LOW)
    return high, (values - high.astype(WIDE)).astype(LOW)


def outer(left, right):
    return lax.dot_general(left, right, (((0,), (0,)), ((), ())), preferred_element_type=WIDE)


def against(left, right):
    return lax.dot_general(left, right, (((1,), (1,)), ((), ())), preferred_element_type=WIDE)


def number(shape, axis):
    return lax.broadcasted_iota(jnp.int32, shape, axis).astype(WIDE)


def low_if(condition):
    return jnp.where(condition, 1.0, 0.0).astype(LOW)


def remainder(values, step):
    return values - step * jnp.floor((values + 0.5) * (1.0 / step))


def owners(shape, slot_axis, chunk):
    offset = number(shape, slot_axis) - chunk * number(shape, 1 - slot_axis)
    return low_if((offset >= 0.0) & (offset < chunk))


def wanted(shape, slot_axis, pad):
    within = remainder(number(shape, slot_axis), 2 * pad)
    left = jnp.where(within < pad, within, -5.0)
    right = jnp.where(within >= pad, within - pad, -5.0)
    return left, right


def token_kernel(
    capacity,
    pad,
    routes_hbm,
    combine_hbm,
    limits_hbm,
    tokens_hbm,
    tok_out,
    rank_out,
    weight_out,
    routes_ref,
    combine_ref,
    limits_ref,
    tokens_ref,
    sems,
):
    copies = [
        pltpu.make_async_copy(source, target, sems.at[at])
        for at, (source, target) in enumerate(
            (
                (routes_hbm, routes_ref),
                (combine_hbm, combine_ref),
                (limits_hbm, limits_ref),
                (tokens_hbm, tokens_ref),
            )
        )
    ]
    for copy in copies:
        copy.start()
    top_count, tok_rows = routes_ref.shape
    experts = limits_ref.shape[1]
    chunk = 2 * pad
    slots = experts * capacity
    owner = owners((slots, experts), 0, capacity)
    place = remainder(number((slots, 1), 0), capacity)
    rows = GROUP * capacity
    moves = [shifts((GROUP * chunk, rows), 1, capacity, pad, side) for side in range(2)]
    before = number((tok_rows, tok_rows), 0) < number((tok_rows, tok_rows), 1)
    square = (experts, experts)
    for copy in copies:
        copy.wait()
    labels = lax.broadcasted_iota(jnp.int32, (experts, tok_rows), 0)
    listed = jnp.zeros((experts, tok_rows), WIDE)
    weight = jnp.zeros((experts, tok_rows), WIDE)
    for entry in range(top_count):
        match = routes_ref[entry : entry + 1, :] == labels
        listed = jnp.where(match, 1.0, listed)
        weight = jnp.where(match, combine_ref[entry : entry + 1, :], weight)
    rank = mul(listed.astype(LOW), low_if(before))
    diagonal = number(square, 0) == number(square, 1)
    bounds = jnp.where(diagonal, limits_ref[...].astype(WIDE), 0.0)
    kept = (listed > 0.0) & (rank < jnp.sum(bounds, axis=1, keepdims=True))
    rank = jnp.where(kept, rank, -1.0)
    rank_out[...] = rank
    weight_out[...] = weight
    picked = low_if(mul(owner, rank.astype(LOW)) == place)
    compact = mul(picked, tokens_ref[...]).astype(LOW)
    lanes = compact.shape[1] // 2
    for at in range(0, experts // GROUP, 2):
        first = compact[at * rows : (at + 1) * rows]
        second = compact[(at + 1) * rows : (at + 2) * rows]
        moved = mul(moves[0], jnp.concatenate([first[:, :lanes], second[:, :lanes]], axis=1))
        moved = moved + mul(
            moves[1], jnp.concatenate([first[:, lanes:], second[:, lanes:]], axis=1)
        )
        for side in range(2):
            tok_out[(at + side) * GROUP : (at + side + 1) * GROUP] = (
                moved[:, side * lanes : (side + 1) * lanes]
                .reshape(GROUP, chunk, lanes)
                .astype(LOW)
            )


def grad_kernel(pad, rank_ref, weight_ref, clip_ref, cot_ref, cot_out):
    experts, tok_rows = rank_ref.shape
    chunk = 2 * pad
    slots = experts * chunk
    owner = owners((slots, experts), 0, chunk)
    left, right = wanted((slots, tok_rows), 0, pad)
    spread = mul(owner, rank_ref[...].astype(LOW))
    high, rest = split_low(weight_ref[...] * clip_ref[...].astype(WIDE))
    high, rest = mul(owner, high), mul(owner, rest)
    coefs = jnp.concatenate(
        [
            jnp.where(spread == place, part, 0.0).astype(LOW)
            for part in (high, rest)
            for place in (left, right)
        ],
        axis=1,
    )
    cot = cot_ref[...]
    lanes = cot.shape[1] // 2
    sides = jnp.concatenate([cot[:, :lanes], cot[:, lanes:]] * 2, axis=0)
    cot_out[...] = mul(coefs, sides).reshape(experts, chunk, lanes).astype(LOW)


def table_kernel(capacity, rank_ref, weight_ref, table_out):
    experts, tok_rows = rank_ref.shape
    slots = experts * capacity
    owner = owners((experts, slots), 1, capacity)
    place = remainder(number((1, slots), 1), capacity)
    picked = mul(rank_ref[...].T.astype(LOW), owner) == place
    table_out[0:tok_rows, :] = low_if(picked)
    for at, part in enumerate(split_low(weight_ref[...].T)):
        table_out[(at + 1) * tok_rows : (at + 2) * tok_rows, :] = jnp.where(
            picked, mul(part, owner), 0.0
        ).astype(LOW)


def places(group, capacity, transposed):
    size = 4 * group * capacity
    chunked = number((1, size) if transposed else (size, 1), 1 if transposed else 0)
    expert = jnp.floor((chunked + 0.5) * (1.0 / (4 * capacity)))
    within = chunked - 4 * capacity * expert
    piece = jnp.floor((within + 0.5) * (1.0 / capacity))
    stacked = within - capacity * piece + capacity * (expert + group * piece)
    return low_if(number((size, size), 0 if transposed else 1) == stacked)


def shifts(shape, row_axis, capacity, pad, side):
    row = number(shape, row_axis)
    block = jnp.floor((row + 0.5) * (1.0 / capacity))
    return low_if(
        number(shape, 1 - row_axis) == row + (2 * pad - capacity) * block + pad * side
    )


GROUP = 8


def unpack_kernel(capacity, pad, core_ref, chunks_ref, keep_out, give_out):
    lanes = chunks_ref.shape[2]
    half = chunks_ref.shape[0] // 2
    rows, slots = GROUP * capacity, GROUP * 2 * pad
    moves = [shifts((rows, slots), 0, capacity, pad, side) for side in range(2)]
    core = core_ref[0]
    for out_ref, base in ((keep_out, core * half), (give_out, (1 - core) * half)):
        for at in range(half // GROUP):
            chunk = chunks_ref[pl.ds(base + at * GROUP, GROUP)].reshape(slots, lanes)
            for side in range(2):
                out_ref[at * rows : (at + 1) * rows, side * lanes : (side + 1) * lanes] = mul(
                    moves[side], chunk
                ).astype(LOW)


def pack_kernel(
    capacity, core_ref, mine_hbm, got_hbm, chunks_out, mine_ref, got_ref, sems
):
    loads = [
        pltpu.make_async_copy(mine_hbm, mine_ref, sems.at[0]),
        pltpu.make_async_copy(got_hbm, got_ref, sems.at[1]),
    ]
    for load in loads:
        load.start()
    lanes = chunks_out.shape[2]
    half = chunks_out.shape[0] // 2
    rows = GROUP * capacity
    moves = places(GROUP, capacity, False)
    core = core_ref[0]
    for in_ref, base, load in (
        (mine_ref, core * half, loads[0]),
        (got_ref, (1 - core) * half, loads[1]),
    ):
        load.wait()
        for at in range(0, half // GROUP, 2):
            stacked = jnp.concatenate(
                [
                    jnp.concatenate(
                        [
                            in_ref[first + now * rows : first + (now + 1) * rows, cols]
                            for now in (at, at + 1)
                        ],
                        axis=1,
                    )
                    for first in (0, half * capacity)
                    for cols in (slice(0, lanes), slice(lanes, 2 * lanes))
                ],
                axis=0,
            )
            moved = mul(moves, stacked)
            for side in range(2):
                chunks_out[pl.ds(base + (at + side) * GROUP, GROUP)] = (
                    moved[:, side * lanes : (side + 1) * lanes]
                    .reshape(GROUP, 4 * capacity, lanes)
                    .astype(LOW)
                )


def merge_kernel(
    capacity,
    chunks_ref,
    table_ref,
    layer_out,
    token_out,
    out_rows,
    grad_rows,
):
    experts, _, lanes = chunks_ref.shape
    tok_rows = layer_out.shape[0]
    rows = GROUP * capacity
    moves = places(GROUP, capacity, True)
    for at in range(0, experts // GROUP, 2):
        chunks = [
            chunks_ref[now * GROUP : (now + 1) * GROUP].reshape(4 * rows, lanes)
            for now in (at, at + 1)
        ]
        pieces = mul(moves, jnp.concatenate(chunks, axis=1)).astype(LOW)
        for piece in range(4):
            target = (out_rows, grad_rows)[piece // 2]
            cols = slice(piece % 2 * lanes, (piece % 2 + 1) * lanes)
            for side in range(2):
                first = (at + side) * rows
                target[first : first + rows, cols] = pieces[
                    piece * rows : (piece + 1) * rows, side * lanes : (side + 1) * lanes
                ]
    sums = mul(table_ref[tok_rows:, :], out_rows[...])
    layer_out[...] = (sums[:tok_rows] + sums[tok_rows:]).astype(LOW)
    token_out[...] = mul(table_ref[0:tok_rows, :], grad_rows[...]).astype(LOW)


def gate_up_kernel(
    keep_ref,
    got_ref,
    gate_ref,
    up_ref,
    other_ref,
    out_hbm,
    out_ref,
    sems,
):
    ff = gate_ref.shape[1]
    step = ff // 3
    copies = []
    keep, got = keep_ref[...], got_ref[...]
    for at in range(6):
        own_ref = (gate_ref, up_ref)[at // 3]
        cols = slice(at * step, (at + 1) * step)
        own_cols = slice(at % 3 * step, (at % 3 + 1) * step)
        out_ref[:, cols] = (mul(keep, own_ref[:, own_cols]) + mul(got, other_ref[:, cols])).astype(
            LOW
        )
        copy = pltpu.make_async_copy(out_ref.at[:, cols], out_hbm.at[:, cols], sems.at[at])
        copy.start()
        copies.append(copy)
    for copy in copies:
        copy.wait()


def hidden_grad_kernel(parity_ref, keep_ref, got_ref, own_ref, other_ref, stay_out, leave_out):
    block = stay_out.shape[1]
    parts = against(keep_ref[...], own_ref[...]) + against(got_ref[...], other_ref[...])
    odd = parity_ref[0] == 1
    for at in range(stay_out.shape[0]):
        first = parts[2 * at * block : (2 * at + 1) * block]
        second = parts[(2 * at + 1) * block : (2 * at + 2) * block]
        stay_out[at] = jnp.where(odd, second, first).astype(LOW)
        leave_out[at] = jnp.where(odd, first, second).astype(LOW)


def total_kernel(parts_ref, out_ref):
    total = parts_ref[0].astype(WIDE)
    for at in range(1, parts_ref.shape[0]):
        total = total + parts_ref[at].astype(WIDE)
    out_ref[...] = total.astype(LOW)


def rows_kernel(
    shares_hbm,
    grad_hbm,
    gu_hbm,
    down_hbm,
    gu_own_hbm,
    down_own_hbm,
    hidden_hbm,
    derived_hbm,
    give_hbm,
    mine_hbm,
    hidden_out,
    derived_out,
    give_out,
    mine_out,
    shares_ref,
    grad_ref,
    gu_ref,
    down_ref,
    gu_own_ref,
    down_own_ref,
    sems,
):
    half, ff = grad_ref.shape
    step = half // 4
    blocks = [slice(at * step, (at + 1) * step) for at in range(4)]
    loads = [
        (
            pltpu.make_async_copy(grad_hbm.at[rows], grad_ref.at[rows], sems.at[6 + at]),
            pltpu.make_async_copy(shares_hbm.at[rows], shares_ref.at[rows], sems.at[at]),
        )
        for at, rows in enumerate(blocks)
    ]
    weights = [
        pltpu.make_async_copy(down_hbm, down_ref, sems.at[4]),
        pltpu.make_async_copy(gu_hbm, gu_ref, sems.at[5]),
        pltpu.make_async_copy(down_own_hbm, down_own_ref, sems.at[10]),
        pltpu.make_async_copy(gu_own_hbm, gu_own_ref, sems.at[11]),
    ]
    for copy in [copy for load in loads for copy in load] + weights:
        copy.start()
    stores = []

    def store(source, target):
        stores.append(pltpu.make_async_copy(source, target, sems.at[12 + len(stores)]))
        stores[-1].start()

    for rows, load in zip(blocks, loads):
        for copy in load:
            copy.wait()
        gate_val = shares_ref[rows, :ff].astype(WIDE)
        up_val = shares_ref[rows, ff:].astype(WIDE)
        grad_hidden = grad_ref[rows, :].astype(WIDE)
        active, slope = swish_parts(gate_val)
        hidden_out[rows, :] = (active * up_val).astype(LOW)
        derived_out[rows, :ff] = (grad_hidden * up_val * slope).astype(LOW)
        derived_out[rows, ff:] = (grad_hidden * active).astype(LOW)
        store(hidden_out.at[rows], hidden_hbm.at[rows])
        store(derived_out.at[rows], derived_hbm.at[rows])
    for copy in weights:
        copy.wait()
    for out_ref, out_hbm, lower_ref, upper_ref in (
        (give_out, give_hbm, down_ref, gu_ref),
        (mine_out, mine_hbm, down_own_ref, gu_own_ref),
    ):
        out_ref[:half, :] = mul(hidden_out[...], lower_ref[...]).astype(LOW)
        store(out_ref.at[:half], out_hbm.at[:half])
        out_ref[half:, :] = against(derived_out[...], upper_ref[...]).astype(LOW)
        store(out_ref.at[half:], out_hbm.at[half:])
    for copy in stores:
        copy.wait()


def body(
    tokens, routes, combine, clip_mask, limits, cotangent, gate_weight, up_weight, down_weight
):
    tok_rows, top_count = routes.shape
    experts = limits.shape[0]
    capacity = 9 * tok_rows * top_count // (8 * experts)
    pad = -(-capacity // 4) * 4
    half = experts * capacity // 2
    width = tokens.shape[1]
    lanes = width // 2
    slots = experts * capacity
    ff = gate_weight.shape[2]
    devices = lax.axis_size("dp")
    chips = devices // 2
    spot = lax.axis_index("dp").astype(jnp.int32)
    core = (spot % 2).reshape(1)
    parity = (spot // 2 % 2).reshape(1)
    column = [[2 * chip + which for chip in range(chips)] for which in range(2)]
    swap_pairs = [(device, device ^ 1) for device in range(devices)]
    near_pairs = []
    for chip in range(chips):
        near_pairs.append((2 * chip, 2 * (chip ^ 1)))
        near_pairs.append((2 * chip + 1, 2 * ((((chip - 1) ^ 1) + 1) % chips) + 1))
    alike = [
        [2 * chip + which for chip in range(first, chips, 2)] for which in range(2) for first in range(2)
    ]
    chunk_shape = jax.ShapeDtypeStruct((experts, 2 * pad, lanes), LOW)
    rank_shape = jax.ShapeDtypeStruct((experts, tok_rows), WIDE)
    half_shape = jax.ShapeDtypeStruct((half, width), LOW)
    tok_shape = jax.ShapeDtypeStruct((tok_rows, width), LOW)
    in_smem = pl.BlockSpec(memory_space=pltpu.SMEM)
    in_vmem = pl.BlockSpec(memory_space=pltpu.VMEM)
    in_hbm = pl.BlockSpec(memory_space=pltpu.HBM)
    anywhere = pl.BlockSpec(memory_space=pl.ANY)
    params = pltpu.CompilerParams(vmem_limit_bytes=16 * 1024 * 1024)

    def swap(values):
        return lax.ppermute(values, "dp", swap_pairs)

    def exchange(chunks):
        return lax.all_to_all(chunks, "expert", split_axis=0, concat_axis=0, tiled=True)

    def unpack(chunks):
        keep, give = pl.pallas_call(
            functools.partial(unpack_kernel, capacity, pad),
            out_shape=(half_shape, half_shape),
            in_specs=[in_smem, in_vmem],
            compiler_params=params,
            name="unpack",
        )(core, chunks)
        return keep, swap(give)

    gate_own, up_own, down_own = gate_weight[0], up_weight[0], down_weight[0]
    gu_own = jnp.concatenate([gate_own, up_own], axis=1)
    gu_other = swap(gu_own)
    down_other = swap(down_own)

    token_send, rank, weight = pl.pallas_call(
        functools.partial(token_kernel, capacity, pad),
        out_shape=(chunk_shape, rank_shape, rank_shape),
        in_specs=[anywhere] * 4,
        scratch_shapes=[
            pltpu.VMEM((top_count, tok_rows), jnp.int32),
            pltpu.VMEM((top_count, tok_rows), WIDE),
            pltpu.VMEM((1, experts), jnp.int32),
            pltpu.VMEM((tok_rows, width), LOW),
            pltpu.SemaphoreType.DMA((4,)),
        ],
        compiler_params=pltpu.CompilerParams(vmem_limit_bytes=63 * 1024 * 1024),
        name="token_rows",
    )(routes.T, combine.T, limits.reshape(1, experts), tokens)
    grad_send = pl.pallas_call(
        functools.partial(grad_kernel, pad),
        out_shape=chunk_shape,
        compiler_params=params,
        name="grad_rows",
    )(rank, weight, clip_mask.reshape(1, tok_rows), cotangent)
    token_chunks, grad_send = lax.optimization_barrier((exchange(token_send), grad_send))
    token_keep, token_got = unpack(token_chunks)
    gate_up = pl.pallas_call(
        gate_up_kernel,
        out_shape=jax.ShapeDtypeStruct((half, 2 * ff), LOW),
        in_specs=[in_vmem] * 5,
        out_specs=in_hbm,
        scratch_shapes=[pltpu.VMEM((half, 2 * ff), LOW), pltpu.SemaphoreType.DMA((6,))],
        compiler_params=params,
        name="gate_up",
    )(token_keep, token_got, gate_own, up_own, gu_other)
    gate_up, grad_send = lax.optimization_barrier((gate_up, grad_send))
    shares = lax.psum_scatter(
        gate_up, "dp", scatter_dimension=0, tiled=True, axis_index_groups=column
    )
    grad_keep, grad_got = unpack(exchange(grad_send))
    part_shape = jax.ShapeDtypeStruct((chips // 2, half // chips, ff), LOW)
    stay, leave = pl.pallas_call(
        hidden_grad_kernel,
        out_shape=(part_shape, part_shape),
        in_specs=[in_smem] + [in_vmem] * 4,
        compiler_params=params,
        name="hidden_grad",
    )(parity, grad_keep, grad_got, down_own, down_other)
    shares, near = lax.optimization_barrier((shares, lax.ppermute(leave, "dp", near_pairs)))
    joined = (stay.astype(WIDE) + near.astype(WIDE)).astype(LOW)
    shares_full = lax.all_gather(shares, "dp", axis=0, tiled=True, axis_index_groups=column)
    grad_parts = lax.all_to_all(
        joined, "dp", split_axis=0, concat_axis=0, tiled=True, axis_index_groups=alike
    )
    grad_total = pl.pallas_call(
        total_kernel,
        out_shape=jax.ShapeDtypeStruct((half // chips, ff), LOW),
        compiler_params=params,
        name="total",
    )(grad_parts)
    grad_full = lax.all_gather(grad_total, "dp", axis=0, tiled=True, axis_index_groups=column)
    pair_shape = jax.ShapeDtypeStruct((2 * half, width), LOW)
    hidden_full, derived_full, give, mine = pl.pallas_call(
        rows_kernel,
        out_shape=(
            jax.ShapeDtypeStruct((half, ff), LOW),
            jax.ShapeDtypeStruct((half, 2 * ff), LOW),
            pair_shape,
            pair_shape,
        ),
        in_specs=[anywhere] * 6,
        out_specs=(anywhere,) * 4,
        scratch_shapes=[
            pltpu.VMEM((half, ff), LOW),
            pltpu.VMEM((half, 2 * ff), LOW),
            pltpu.VMEM((2 * half, width), LOW),
            pltpu.VMEM((2 * half, width), LOW),
            pltpu.VMEM((half, 2 * ff), LOW),
            pltpu.VMEM((half, ff), LOW),
            pltpu.VMEM((width, 2 * ff), LOW),
            pltpu.VMEM((ff, width), LOW),
            pltpu.VMEM((width, 2 * ff), LOW),
            pltpu.VMEM((ff, width), LOW),
            pltpu.SemaphoreType.DMA((24,)),
        ],
        compiler_params=pltpu.CompilerParams(vmem_limit_bytes=63 * 1024 * 1024),
        name="expert_rows",
    )(shares_full, grad_full, gu_other, down_other, gu_own, down_own)
    back = exchange(
        pl.pallas_call(
            functools.partial(pack_kernel, capacity),
            out_shape=jax.ShapeDtypeStruct((experts, 4 * capacity, lanes), LOW),
            in_specs=[in_smem] + [anywhere] * 2,
            scratch_shapes=[
                pltpu.VMEM((2 * half, width), LOW),
                pltpu.VMEM((2 * half, width), LOW),
                pltpu.SemaphoreType.DMA((2,)),
            ],
            compiler_params=pltpu.CompilerParams(vmem_limit_bytes=63 * 1024 * 1024),
            name="pack",
        )(core, mine, swap(give))
    )

    lower_got = swap(outer(hidden_full, grad_got).astype(LOW))
    down_grads = (outer(hidden_full, grad_keep) + lower_got.astype(WIDE)).astype(LOW)
    upper_got = swap(outer(token_got, derived_full).astype(LOW)).astype(WIDE)
    gate_grads = (outer(token_keep, derived_full[:, :ff]) + upper_got[:, :ff]).astype(LOW)
    up_grads = (outer(token_keep, derived_full[:, ff:]) + upper_got[:, ff:]).astype(LOW)

    table = pl.pallas_call(
        functools.partial(table_kernel, capacity),
        out_shape=jax.ShapeDtypeStruct((3 * tok_rows, slots), LOW),
        compiler_params=params,
        name="table",
    )(rank, weight)
    rows_scratch = pltpu.VMEM((slots, width), LOW)
    layer_out, token_grads = pl.pallas_call(
        functools.partial(merge_kernel, capacity),
        out_shape=(tok_shape, tok_shape),
        scratch_shapes=[rows_scratch, rows_scratch],
        compiler_params=params,
        name="merge",
    )(back, table)
    return (layer_out, token_grads, gate_grads[None], up_grads[None], down_grads[None])


def solution(mesh):
    in_specs = (
        P("expert", "dp"),
        P("expert", None),
        P("expert", None),
        P("expert"),
        P(),
        P("expert", "dp"),
        P("expert", "dp", None),
        P("expert", "dp", None),
        P("expert", None, "dp"),
    )
    out_specs = (
        P("expert", "dp"),
        P("expert", "dp"),
        P("expert", "dp", None),
        P("expert", "dp", None),
        P("expert", None, "dp"),
    )
    return jax.shard_map(body, mesh=mesh, in_specs=in_specs, out_specs=out_specs, check_vma=False)
```
